128 devices in a mesh: chan: 8 (over x, core), row: 16 (over z, y).
Axes of the slice: x: 4, y: 4, z: 4, core: 2. Of those that a mesh axis runs over, the one named last changes fastest.
Arguments:
- voltages: bfloat16 [8, 16, 2, 32768], P(None, None, None, 'chan'), may hold values from -6 to 6
- kernel: float32 [8, 4, 4], P('chan'), may hold values from 0.25 to 1.5
- route_lists: int32 [8, 16, 512], P(None, 'row'), may hold values from 0 to 4095, as said below
- row_members: int32 [1024, 64], P('row'), may hold values from 0 to 4095, as said below
- row_counts: int32 [1024], P('row'), may hold values from 0 to 64, as said below
- anchor_cols: int32 [1024, 64], P('row'), may hold values from 0 to 1023, as said below
Outputs:
- sky: float32 [8, 1024, 1024], P('chan', None, 'row')
The draws below stay inside these ranges and needn't reach their ends.
Inputs may be any that keep to these rules, and one draw needn't show every extreme that they name: `route_lists`: in each group and slab the listed entries name dipoles of the group; the entries that some row_members entry below its count points to are distinct dipoles, and no dipole is pointed to from two slabs. In every draw one slab is named in all 512 slots of every group's list and gridded from all of them; the other slabs use fewer. `row_members`: entries below the row's count are slots of the row's slab, distinct over the whole slab; entries at and after the count name other slots of the same slab. `row_counts`: in every draw all 64 rows of one slab hold 64 dipoles. `anchor_cols`: the 64 columns of one row are distinct; kernel cells past the last column fall outside the grid.
All inputs are finite; a program needn't handle non-finite values.
Results may differ from the reference program's by a relative error of at most 0.0015.
Values may be sent and summed in bfloat16 or wider, within the bound.
No kernel may reach another device: no remote copies, remote signals or barrier semaphores. Data moves between devices by JAX's collectives and lax.ppermute only.
A program may use at most 128 MiB of HBM per device.

```python
import math
import jax
import jax.numpy as jnp
from jax import lax

NGRID = 1024
KERNEL_SIDE = 4
TIME_SAMPLES = 16
DIPOLES_PER_SET = 4096
DIPOLE_TOTAL = 32768
FREQ_CHANNELS = 8
SLAB = 64
SLAB_LIST_LIMIT = 512
SLOTS = 4096
ROW_CAP = 64
N_CHAN = 8
N_ROW = 16


def layout(key):
    weight_key, core_key, cell_key, column_key, group_key = jax.random.split(key, 5)
    core_slab = jax.random.randint(core_key, (), 0, N_ROW)
    kernel_weights = jax.random.randint(weight_key, (N_CHAN, N_ROW), 1, 4)
    slab_index = jnp.arange(N_ROW, dtype=jnp.int32)
    kernel_weights = jnp.where(slab_index[None, :] == core_slab, 3 * N_ROW, kernel_weights)
    occupied_slots = jnp.minimum(SLAB_LIST_LIMIT, DIPOLES_PER_SET * kernel_weights // jnp.sum(kernel_weights, axis=1, keepdims=True))
    start_positions = jnp.cumsum(occupied_slots, axis=1) - occupied_slots
    dipole_set_keys = jax.random.split(group_key, N_CHAN)
    dipole_set_order = jax.vmap(lambda single_key: jax.random.permutation(single_key, DIPOLES_PER_SET))(dipole_set_keys)
    slot_numbers = jnp.arange(SLAB_LIST_LIMIT, dtype=jnp.int32)
    dipole_location = (start_positions[:, :, None] + slot_numbers[None, None, :]) % DIPOLES_PER_SET
    routes = jax.vmap(lambda perm_row, pos_rows: perm_row[pos_rows])(dipole_set_order, dipole_location).astype(jnp.int32)
    valid_slot = slot_numbers[None, None, :] < occupied_slots[:, :, None]
    valid_by_slab = jnp.transpose(valid_slot, (1, 0, 2)).reshape(N_ROW, SLOTS)
    cell_keys = jax.random.split(cell_key, N_ROW)
    slot_of_cell = jax.vmap(lambda single_key: jax.random.permutation(single_key, SLOTS))(cell_keys)
    valid_cell = jnp.take_along_axis(valid_by_slab, slot_of_cell, axis=1)
    rows_slot = slot_of_cell.reshape(NGRID, ROW_CAP).astype(jnp.int32)
    rows_valid = valid_cell.reshape(NGRID, ROW_CAP).astype(jnp.int32)
    ordering = jnp.argsort(1 - rows_valid, axis=1, stable=True)
    members = jnp.take_along_axis(rows_slot, ordering, axis=1).astype(jnp.int32)
    counts = jnp.sum(rows_valid, axis=1).astype(jnp.int32)
    column_keys = jax.random.split(column_key, NGRID)
    columns = jax.vmap(lambda single_key: jax.random.permutation(single_key, NGRID)[:ROW_CAP])(column_keys).astype(jnp.int32)
    return (routes, members, counts, columns)


def draw_route_lists(key, part):
    return layout(key)[0]


def draw_row_members(key, part):
    return layout(key)[1]


def draw_row_counts(key, part):
    return layout(key)[2]


def draw_anchor_cols(key, part):
    return layout(key)[3]


def level_of(own_key, shape, cuts, smallest, top_value):
    def one(dim, blocks):
        steps = jax.random.uniform(jax.random.fold_in(jax.random.fold_in(own_key, 6), dim), (blocks,), jnp.float32, smallest / len(cuts), top_value / len(cuts))
        return jnp.repeat(jnp.exp(steps), shape[dim] // blocks).reshape((-1,) + (1,) * (len(shape) - dim - 1))

    factor_of = one(*cuts[0])
    for cut in cuts[1:]:
        factor_of = factor_of * one(*cut)
    return factor_of


def scatter_about(own_key, shape, deviation, bound, shards=(), kind=jnp.bfloat16):
    array = deviation * jax.random.normal(own_key, shape, jnp.float32)
    if shards:
        array = array * level_of(own_key, shape, shards, -0.22, 0.18)
    return jnp.clip(array, -bound, bound).astype(kind)


def setup_inputs(seed: int = 0) -> dict:
    streams_of = jax.random.split(jax.random.key(seed), 7)
    voltages = scatter_about(streams_of[0], (FREQ_CHANNELS, TIME_SAMPLES, 2, DIPOLE_TOTAL), 1.0, 6.0, ((3, 8),))
    kernel = jnp.clip(0.25 + 1.25 * jax.random.uniform(streams_of[1], (FREQ_CHANNELS, KERNEL_SIDE, KERNEL_SIDE), jnp.float32) ** level_of(streams_of[1], (FREQ_CHANNELS, KERNEL_SIDE, KERNEL_SIDE), ((0, 8),), -0.2, 0.2), 0.25, 1.5)
    route_lists = draw_route_lists(jax.random.fold_in(streams_of[6], 71), 0)
    row_members = draw_row_members(jax.random.fold_in(streams_of[6], 71), 0)
    row_counts = draw_row_counts(jax.random.fold_in(streams_of[6], 71), 0)
    anchor_cols = draw_anchor_cols(jax.random.fold_in(streams_of[6], 71), 0)
    return dict(voltages=voltages, kernel=kernel, route_lists=route_lists, row_members=row_members, row_counts=row_counts, anchor_cols=anchor_cols)


def twiddle_tables(length):
    product = (jnp.arange(length, dtype=jnp.int32)[:, None] * jnp.arange(length, dtype=jnp.int32)[None, :]) % length
    angles = product.astype(jnp.float32) * (-2.0 * math.pi / length)
    return jnp.cos(angles).astype(jnp.bfloat16), jnp.sin(angles).astype(jnp.bfloat16)


def reference(voltages, kernel, route_lists, row_members, row_counts, anchor_cols):
    start_positions = jnp.arange(N_CHAN, dtype=jnp.int32)[:, None, None] * DIPOLES_PER_SET
    slab_ids = jnp.transpose(route_lists + start_positions, (1, 0, 2)).reshape(-1)
    row_slab = jnp.arange(NGRID, dtype=jnp.int32) // SLAB
    antenna_ids = jnp.take(slab_ids, (row_slab[:, None] * SLOTS + row_members).astype(jnp.int32))
    is_live = jnp.arange(ROW_CAP, dtype=jnp.int32)[None, :] < row_counts[:, None]
    row_index = jnp.broadcast_to(jnp.arange(NGRID, dtype=jnp.int32)[:, None], (NGRID, ROW_CAP))
    scale_factor = 1.0 / (DIPOLE_TOTAL * TIME_SAMPLES * KERNEL_SIDE * KERNEL_SIDE)
    twiddle_cos, twiddle_sin = twiddle_tables(NGRID)
    cos_wide = twiddle_cos.astype(jnp.float32)
    sin_wide = twiddle_sin.astype(jnp.float32)

    def one_channel(inputs):
        volts, kernel_taps = inputs
        chosen = jnp.take(volts, antenna_ids, axis=2).astype(jnp.float32)
        chosen = jnp.where(is_live, chosen, jnp.float32(0.0))
        anchored = jnp.zeros((TIME_SAMPLES, 2, NGRID, NGRID), jnp.float32).at[:, :, row_index, anchor_cols].add(chosen)
        padded = jnp.pad(anchored, ((0, 0), (0, 0), (KERNEL_SIDE - 1, 0), (KERNEL_SIDE - 1, 0)))
        aperture = jnp.zeros((TIME_SAMPLES, 2, NGRID, NGRID), jnp.float32)
        for tap_row in range(KERNEL_SIDE):
            for tap_col in range(KERNEL_SIDE):
                window = padded[:, :, KERNEL_SIDE - 1 - tap_row:KERNEL_SIDE - 1 - tap_row + NGRID, KERNEL_SIDE - 1 - tap_col:KERNEL_SIDE - 1 - tap_col + NGRID]
                aperture = aperture + kernel_taps[tap_row, tap_col] * window
        aperture = aperture.astype(jnp.bfloat16)
        real_flat = aperture[:, 0].reshape(TIME_SAMPLES * NGRID, NGRID)
        imag_flat = aperture[:, 1].reshape(TIME_SAMPLES * NGRID, NGRID)
        spec_real = jnp.dot(real_flat, twiddle_cos, preferred_element_type=jnp.float32) - jnp.dot(imag_flat, twiddle_sin, preferred_element_type=jnp.float32)
        spec_imag = jnp.dot(real_flat, twiddle_sin, preferred_element_type=jnp.float32) + jnp.dot(imag_flat, twiddle_cos, preferred_element_type=jnp.float32)
        spec_real = spec_real.astype(jnp.bfloat16).astype(jnp.float32).reshape(TIME_SAMPLES, NGRID, NGRID)
        spec_imag = spec_imag.astype(jnp.bfloat16).astype(jnp.float32).reshape(TIME_SAMPLES, NGRID, NGRID)
        image_real = jnp.einsum("yw,tyu->twu", cos_wide, spec_real) - jnp.einsum("yw,tyu->twu", sin_wide, spec_imag)
        image_imag = jnp.einsum("yw,tyu->twu", sin_wide, spec_real) + jnp.einsum("yw,tyu->twu", cos_wide, spec_imag)
        power_terms = image_real * image_real + image_imag * image_imag
        return (jnp.sum(power_terms, axis=0) * scale_factor).astype(jnp.float32)

    return lax.map(one_channel, (voltages, kernel))
```

```python
import jax
import jax.numpy as jnp
import numpy as np
from jax import lax
from jax.experimental import pallas as pl
from jax.experimental.pallas import tpu as pltpu
from jax.sharding import PartitionSpec as P

NGRID = 1024
KERNEL_SIDE = 4
RADIX = 4
POINTS = NGRID // RADIX
LANES = 128
F32 = jnp.float32
BF16 = jnp.bfloat16


def stage_tables():
    n = np.arange(NGRID, dtype=np.int64)
    product = (n[:, None] * n[None, :POINTS]) % NGRID
    angles = product.astype(np.float32) * np.float32(-2.0 * np.pi / NGRID)
    cos = np.cos(angles).astype(np.float32)
    sin = np.sin(angles).astype(np.float32)
    parts = []
    for q in range(RADIX):
        c, s = cos[q::RADIX], sin[q::RADIX]
        parts.append(np.block([[c, s], [-s, c]]))
    table = np.stack(parts)
    return (
        np.ascontiguousarray(table.transpose(0, 2, 1)).astype(jnp.bfloat16),
        table.astype(jnp.bfloat16),
    )


def butterfly(re, im):
    ra, rb = re[0] + re[2], re[0] - re[2]
    rc, rd = re[1] + re[3], re[1] - re[3]
    ia, ib = im[0] + im[2], im[0] - im[2]
    ic, id_ = im[1] + im[3], im[1] - im[3]
    return (ra + rc, rb + id_, ra - rc, rb - id_), (ia + ic, ib - rd, ia - ic, ib + rd)


def lookup(rows_of, index, count):
    lane = index & (LANES - 1)
    row = index >> 7
    first = jnp.zeros(index.shape, F32)
    second = jnp.zeros(index.shape, F32)
    for k in range(count):
        a, b = rows_of(k)
        hit = row == k
        a = jnp.take_along_axis(a, lane, axis=1, mode="promise_in_bounds")
        b = jnp.take_along_axis(b, lane, axis=1, mode="promise_in_bounds")
        first = jnp.where(hit, a, first)
        second = jnp.where(hit, b, second)
    return first, second


def sample_kernel(
    taps, volts, lists, wide, tall, power, table, slots, dense, aperture, spectrum
):
    slabs = lists.shape[0]
    groups = volts.shape[0]
    slab_points = POINTS // slabs

    for g in range(groups):
        for i in range(2):
            table[i, :, g, :] = volts[g, i].astype(F32)
    for i in range(2):
        for qy in range(RADIX):
            for qx in range(RADIX):
                for w in range(2):
                    dense[i, qy, qx, w, 0:8, :] = jnp.zeros((8, LANES), F32)

    sub = lax.broadcasted_iota(jnp.int32, (8, LANES), 0)
    lane = lax.broadcasted_iota(jnp.int32, (8, LANES), 1)
    half = (lane >= 64).astype(jnp.int32)
    own_row = [sub == 2 * s + half for s in range(4)]
    cell = lax.broadcasted_iota(jnp.int32, (POINTS, 4 * LANES), 0).astype(BF16)

    def grid_slab(r, carry):
        routes = lists[r, 0].astype(jnp.int32)
        members = lists[r, 1].astype(jnp.int32)
        columns = lists[r, 2].astype(jnp.int32)

        def group_rows(k):
            return tuple(
                jnp.broadcast_to(table[i, k][None], (4, 8, LANES)).reshape(32, LANES)
                for i in range(2)
            )

        slot_re, slot_im = lookup(group_rows, routes, 32)
        slots[0] = slot_re
        slots[1] = slot_im

        def slot_rows(k):
            return tuple(
                jnp.broadcast_to(slots[i, k : k + 1, :], (32, LANES)) for i in range(2)
            )

        values = lookup(slot_rows, members, 32)
        phase = columns & (RADIX - 1)
        point = (columns >> 2).astype(F32)
        for qy in range(RADIX):
            part = slice(8 * qy, 8 * qy + 8)
            planes = [
                jnp.where(phase[part] == qx, values[i][part], 0.0)
                for qx in range(RADIX)
                for i in range(2)
            ]
            for h in range(2):
                left = jnp.concatenate(
                    [
                        jnp.concatenate(
                            [
                                jnp.where(
                                    own_row[s],
                                    jnp.broadcast_to(
                                        plane[4 * h + s : 4 * h + s + 1, :], (8, LANES)
                                    ),
                                    0.0,
                                )
                                for s in range(4)
                            ],
                            axis=1,
                        )
                        for plane in planes
                    ],
                    axis=0,
                ).astype(BF16)
                spot = jnp.concatenate(
                    [
                        point[8 * qy + 4 * h + s : 8 * qy + 4 * h + s + 1, :]
                        for s in range(4)
                    ],
                    axis=1,
                ).astype(BF16)
                onehot = jnp.where(cell == spot, BF16(1), BF16(0))
                placed = lax.dot_general(
                    left, onehot, (((1,), (1,)), ((), ())), preferred_element_type=F32
                )
                start = pl.multiple_of(8 + r * slab_points + 8 * h, 8)
                for qx in range(RADIX):
                    for i in range(2):
                        at = (qx * 2 + i) * 8
                        for w in range(2):
                            dense[i, qy, qx, w, pl.ds(start, 8), :] = placed[
                                at : at + 8, w * LANES : (w + 1) * LANES
                            ]
        return carry

    lax.fori_loop(0, slabs, grid_slab, 0)

    first_lane = lax.broadcasted_iota(jnp.int32, (16, POINTS), 1) == 0

    def convolve(t, carry):
        for i in range(2):
            for qy in range(RADIX):
                sums = [jnp.zeros((16, POINTS), F32) for _ in range(RADIX)]
                for ky in range(KERNEL_SIDE):
                    source = (qy - ky) % RADIX
                    start = 8 + 16 * t - (1 if ky > qy else 0)
                    here = [
                        jnp.concatenate(
                            [
                                dense[i, source, qx, w, pl.ds(start, 16), :]
                                for w in range(2)
                            ],
                            axis=1,
                        )
                        for qx in range(RADIX)
                    ]
                    before = [
                        None
                        if qx == 0
                        else jnp.where(first_lane, 0.0, pltpu.roll(here[qx], 1, 1))
                        for qx in range(RADIX)
                    ]
                    for qx in range(RADIX):
                        for kx in range(KERNEL_SIDE):
                            near = before if kx > qx else here
                            sums[qx] = (
                                sums[qx] + taps[ky, kx] * near[(qx - kx) % RADIX]
                            )
                row = pl.multiple_of(qy * POINTS + 16 * t, 16)
                for qx in range(RADIX):
                    at = (2 * qx + i) * POINTS
                    aperture[pl.ds(row, 16), at : at + POINTS] = sums[qx].astype(BF16)
        return carry

    lax.fori_loop(0, POINTS // 16, convolve, 0)

    def row_transform(qy, carry):
        rows = pl.ds(pl.multiple_of(qy * POINTS, POINTS), POINTS)
        parts = [
            lax.dot_general(
                wide[q],
                aperture[rows, 2 * q * POINTS : 2 * (q + 1) * POINTS],
                (((1,), (1,)), ((), ())),
                preferred_element_type=F32,
            )
            for q in range(RADIX)
        ]
        re, im = butterfly(
            [part[:POINTS] for part in parts], [part[POINTS:] for part in parts]
        )
        at = pl.multiple_of(qy * 2 * POINTS, 2 * POINTS)
        for m in range(RADIX):
            spectrum[m * POINTS : (m + 1) * POINTS, pl.ds(at, POINTS)] = re[m].astype(
                BF16
            )
            spectrum[
                m * POINTS : (m + 1) * POINTS, pl.ds(at + POINTS, POINTS)
            ] = im[m].astype(BF16)
        return carry

    lax.fori_loop(0, RADIX, row_transform, 0)

    def column_transform(n, carry):
        rows = pl.ds(pl.multiple_of(n * 128, 128), 128)
        parts = [
            jnp.dot(
                spectrum[rows, 2 * q * POINTS : 2 * (q + 1) * POINTS],
                tall[q],
                preferred_element_type=F32,
            )
            for q in range(RADIX)
        ]
        re, im = butterfly(
            [part[:, :POINTS] for part in parts], [part[:, POINTS:] for part in parts]
        )
        for m in range(RADIX):
            power[rows, m * POINTS : (m + 1) * POINTS] = (
                re[m] * re[m] + im[m] * im[m]
            ).astype(BF16)
        return carry

    lax.fori_loop(0, NGRID // 128, column_transform, 0)


def sample_power(taps, volts, lists, wide, tall, interpret=False):
    return pl.pallas_call(
        sample_kernel,
        out_shape=jax.ShapeDtypeStruct((NGRID, NGRID), BF16),
        in_specs=[pl.BlockSpec(memory_space=pltpu.SMEM)]
        + [pl.BlockSpec(memory_space=pltpu.VMEM)] * 4,
        out_specs=pl.BlockSpec(memory_space=pltpu.VMEM),
        scratch_shapes=[
            pltpu.VMEM((2, 32, 8, LANES), F32),
            pltpu.VMEM((2, 32, LANES), F32),
            pltpu.VMEM((2, RADIX, RADIX, 2, POINTS + 8, LANES), F32),
            pltpu.VMEM((NGRID, 2 * NGRID), BF16),
            pltpu.VMEM((NGRID, 2 * NGRID), BF16),
        ],
        compiler_params=pltpu.CompilerParams(vmem_limit_bytes=56 * 2**20),
        interpret=interpret,
    )(taps, volts, lists, wide, tall)


def slab_lists(route_lists, row_members, row_counts, anchor_cols):
    routes = route_lists[:, 0, :].reshape(8, 4, LANES).transpose(1, 0, 2)
    slot = ((row_members >> 7) & 3) * 1024 + (row_members >> 9) * LANES
    slot = slot + (row_members & (LANES - 1))
    live = jnp.arange(row_members.shape[1], dtype=jnp.int32)[None, :] < row_counts[:, None]
    slot = jnp.where(live, slot, -1)
    by_phase = [
        a.reshape(-1, RADIX, a.shape[1]).transpose(1, 0, 2).reshape(32, LANES)
        for a in (slot, anchor_cols)
    ]
    return jnp.stack([routes.reshape(32, LANES), *by_phase]).astype(jnp.int16)


def per_device(voltages, kernel, route_lists, row_members, row_counts, anchor_cols):
    chan_count = lax.axis_size("chan")
    row_count = lax.axis_size("row")
    group_size = voltages.shape[3]
    samples = voltages.shape[1]
    lists = slab_lists(route_lists, row_members, row_counts, anchor_cols)
    lists = jnp.broadcast_to(lists[None], (row_count,) + lists.shape)
    lists = lax.all_to_all(lists, "row", split_axis=0, concat_axis=0, tiled=True)
    mine = lax.dynamic_index_in_dim(voltages, lax.axis_index("row"), 1, keepdims=False)
    mine = mine.reshape(chan_count, 2, group_size // LANES, LANES)
    volts = lax.all_to_all(mine, "chan", split_axis=0, concat_axis=0, tiled=True)
    wide, tall = stage_tables()
    power = sample_power(kernel[0], volts, lists, jnp.asarray(wide), jnp.asarray(tall))
    power = power.reshape(row_count, NGRID // row_count, NGRID)
    power = lax.all_to_all(power, "row", split_axis=0, concat_axis=0, tiled=True)
    scale_factor = 1.0 / (group_size * chan_count * samples * KERNEL_SIDE * KERNEL_SIDE)
    sky_image = jnp.sum(power.astype(F32), axis=0) * scale_factor
    return sky_image.T[None]


def solution(mesh):
    in_specs = (
        P(None, None, None, "chan"),
        P("chan", None, None),
        P(None, "row", None),
        P("row", None),
        P("row"),
        P("row", None),
    )
    out_specs = P("chan", None, "row")
    return jax.shard_map(
        per_device, mesh=mesh, in_specs=in_specs, out_specs=out_specs, check_vma=False
    )
```

```python
import jax
import jax.numpy as jnp
import numpy as np
from jax import lax
from jax.experimental import pallas as pl
from jax.experimental.pallas import tpu as pltpu
from jax.sharding import PartitionSpec as P

NGRID = 1024
KERNEL_SIDE = 4
RADIX = 4
POINTS = NGRID // RADIX
LANES = 128
F32 = jnp.float32
BF16 = jnp.bfloat16


def stage_tables():
    n = np.arange(NGRID, dtype=np.int64)
    product = (n[:, None] * n[None, :POINTS]) % NGRID
    angles = product.astype(np.float32) * np.float32(-2.0 * np.pi / NGRID)
    cos = np.cos(angles).astype(np.float32)
    sin = np.sin(angles).astype(np.float32)
    parts = []
    for q in range(RADIX):
        c, s = cos[q::RADIX], sin[q::RADIX]
        parts.append(np.block([[c, s], [-s, c]]))
    table = np.stack(parts)
    return (
        np.ascontiguousarray(table.transpose(0, 2, 1)).astype(jnp.bfloat16),
        table.astype(jnp.bfloat16),
    )


def butterfly(re, im):
    ra, rb = re[0] + re[2], re[0] - re[2]
    rc, rd = re[1] + re[3], re[1] - re[3]
    ia, ib = im[0] + im[2], im[0] - im[2]
    ic, id_ = im[1] + im[3], im[1] - im[3]
    return (ra + rc, rb + id_, ra - rc, rb - id_), (ia + ic, ib - rd, ia - ic, ib + rd)


def pick(table_rows, index):
    return jnp.take_along_axis(table_rows, index, axis=1, mode="promise_in_bounds")


def sample_kernel(
    taps, volts, lists, wide, tall, power, table, slots, dense, aperture, spectrum
):
    slabs = lists.shape[0]
    groups = volts.shape[0]
    slab_points = POINTS // slabs

    for g in range(groups):
        for i in range(2):
            table[i, :, g, :] = volts[g, i].astype(F32)
    for i in range(2):
        for qy in range(RADIX):
            for qx in range(RADIX):
                for w in range(2):
                    dense[i, qy, qx, w, 0:8, :] = jnp.zeros((8, LANES), F32)

    sub = lax.broadcasted_iota(jnp.int32, (8, LANES), 0)
    lane = lax.broadcasted_iota(jnp.int32, (8, LANES), 1)
    own_row = sub == lane >> 4

    def grid_chunks(r, chunks, list_chunks):
        size = 8 * chunks
        routes = lists[r, 0].astype(jnp.int32)
        members = lists[r, 1].astype(jnp.int32)[:size]
        columns = lists[r, 2].astype(jnp.int32)[:size]
        member_lane = members & (LANES - 1)
        member_row = members >> 7
        for s in range(4):
            slots[2, 8 * s : 8 * s + 8, :] = routes[8 * s : 8 * s + 8].astype(F32)

        def list_chunk(s, found):
            route = slots[2, pl.ds(pl.multiple_of(8 * s, 8), 8), :].astype(jnp.int32)
            route_lane = route & (LANES - 1)
            route_row = route >> 7
            slot = [jnp.zeros((8, LANES), F32) for _ in range(2)]
            for k in range(32):
                hit = route_row == k
                slot = [
                    jnp.where(hit, pick(table[i, k], route_lane), slot[i])
                    for i in range(2)
                ]
            found = list(found)
            for i in range(2):
                slots[i, 0:8, :] = slot[i]
            for k in range(8):
                hit = member_row == 8 * s + k
                for i in range(2):
                    row = jnp.broadcast_to(slots[i, k : k + 1, :], (size, LANES))
                    found[i] = jnp.where(hit, pick(row, member_lane), found[i])
            return tuple(found)

        nothing = jnp.zeros((size, LANES), F32)
        values = lax.fori_loop(0, list_chunks, list_chunk, (nothing, nothing))
        columns = columns & (NGRID - 1)
        kind = (columns & (RADIX - 1)) + RADIX * (columns >> 9)
        point = ((columns >> 2) & (LANES - 1)).astype(F32)
        planes = [
            jnp.where(kind == half * RADIX + qx, values[i], 0.0)
            for half in range(2)
            for qx in range(RADIX)
            for i in range(2)
        ]
        cell = lax.broadcasted_iota(jnp.int32, (LANES, chunks * LANES), 0).astype(BF16)
        for qy in range(RADIX):
            for h in range(2):
                at = [8 * c + 2 * qy + h for c in range(chunks)]
                left = jnp.concatenate(
                    [
                        jnp.concatenate(
                            [
                                jnp.where(
                                    own_row,
                                    jnp.broadcast_to(plane[a : a + 1, :], (8, LANES)),
                                    0.0,
                                )
                                for a in at
                            ],
                            axis=1,
                        )
                        for plane in planes
                    ],
                    axis=0,
                ).astype(BF16)
                spot = jnp.concatenate([point[a : a + 1, :] for a in at], axis=1)
                onehot = jnp.where(cell == spot.astype(BF16), BF16(1), BF16(0))
                placed = lax.dot_general(
                    left, onehot, (((1,), (1,)), ((), ())), preferred_element_type=F32
                )
                start = pl.multiple_of(8 + r * slab_points + 8 * h, 8)
                for half in range(2):
                    for qx in range(RADIX):
                        for i in range(2):
                            a = ((half * RADIX + qx) * 2 + i) * 8
                            dense[i, qy, qx, half, pl.ds(start, 8), :] = placed[
                                a : a + 8, :
                            ]

    def grid_slab(r, carry):
        extent = lists[r, 2, 0:16, :].astype(jnp.int32)[0, 0] >> 10
        row_chunks = extent & 3
        list_chunks = (extent >> 2) + 1
        for low, high in ((0, 1), (1, 2), (2, 4)):

            @pl.when((row_chunks >= low) & (row_chunks < high))
            def _():
                grid_chunks(r, high, list_chunks)

        return carry

    lax.fori_loop(0, slabs, grid_slab, 0)

    first_lane = lax.broadcasted_iota(jnp.int32, (16, POINTS), 1) == 0

    def convolve(t, carry):
        for i in range(2):
            for qy in range(RADIX):
                sums = [jnp.zeros((16, POINTS), F32) for _ in range(RADIX)]
                for ky in range(KERNEL_SIDE):
                    source = (qy - ky) % RADIX
                    start = 8 + 16 * t - (1 if ky > qy else 0)
                    here = [
                        jnp.concatenate(
                            [
                                dense[i, source, qx, w, pl.ds(start, 16), :]
                                for w in range(2)
                            ],
                            axis=1,
                        )
                        for qx in range(RADIX)
                    ]
                    before = [
                        None
                        if qx == 0
                        else jnp.where(first_lane, 0.0, pltpu.roll(here[qx], 1, 1))
                        for qx in range(RADIX)
                    ]
                    for qx in range(RADIX):
                        for kx in range(KERNEL_SIDE):
                            near = before if kx > qx else here
                            sums[qx] = (
                                sums[qx] + taps[ky, kx] * near[(qx - kx) % RADIX]
                            )
                row = pl.multiple_of(qy * POINTS + 16 * t, 16)
                for qx in range(RADIX):
                    at = (2 * qx + i) * POINTS
                    aperture[pl.ds(row, 16), at : at + POINTS] = sums[qx].astype(BF16)
        return carry

    lax.fori_loop(0, POINTS // 16, convolve, 0)

    def row_transform(qy, carry):
        rows = pl.ds(pl.multiple_of(qy * POINTS, POINTS), POINTS)
        parts = [
            lax.dot_general(
                wide[q],
                aperture[rows, 2 * q * POINTS : 2 * (q + 1) * POINTS],
                (((1,), (1,)), ((), ())),
                preferred_element_type=F32,
            )
            for q in range(RADIX)
        ]
        re, im = butterfly(
            [part[:POINTS] for part in parts], [part[POINTS:] for part in parts]
        )
        at = pl.multiple_of(qy * 2 * POINTS, 2 * POINTS)
        for m in range(RADIX):
            spectrum[m * POINTS : (m + 1) * POINTS, pl.ds(at, POINTS)] = re[m].astype(
                BF16
            )
            spectrum[
                m * POINTS : (m + 1) * POINTS, pl.ds(at + POINTS, POINTS)
            ] = im[m].astype(BF16)
        return carry

    lax.fori_loop(0, RADIX, row_transform, 0)

    def column_transform(n, carry):
        rows = pl.ds(pl.multiple_of(n * 128, 128), 128)
        parts = [
            jnp.dot(
                spectrum[rows, 2 * q * POINTS : 2 * (q + 1) * POINTS],
                tall[q],
                preferred_element_type=F32,
            )
            for q in range(RADIX)
        ]
        re, im = butterfly(
            [part[:, :POINTS] for part in parts], [part[:, POINTS:] for part in parts]
        )
        for m in range(RADIX):
            power[rows, m * POINTS : (m + 1) * POINTS] = (
                re[m] * re[m] + im[m] * im[m]
            ).astype(BF16)
        return carry

    lax.fori_loop(0, NGRID // 128, column_transform, 0)


def sample_power(taps, volts, lists, wide, tall, interpret=False):
    return pl.pallas_call(
        sample_kernel,
        out_shape=jax.ShapeDtypeStruct((NGRID, NGRID), BF16),
        in_specs=[pl.BlockSpec(memory_space=pltpu.SMEM)]
        + [pl.BlockSpec(memory_space=pltpu.VMEM)] * 4,
        out_specs=pl.BlockSpec(memory_space=pltpu.VMEM),
        scratch_shapes=[
            pltpu.VMEM((2, 32, 8, LANES), F32),
            pltpu.VMEM((3, 32, LANES), F32),
            pltpu.VMEM((2, RADIX, RADIX, 2, POINTS + 8, LANES), F32),
            pltpu.VMEM((NGRID, 2 * NGRID), BF16),
            pltpu.VMEM((NGRID, 2 * NGRID), BF16),
        ],
        compiler_params=pltpu.CompilerParams(vmem_limit_bytes=56 * 2**20),
        interpret=interpret,
    )(taps, volts, lists, wide, tall)


def slab_lists(route_lists, row_members, row_counts, anchor_cols):
    routes = route_lists[:, 0, :].reshape(8, 4, LANES).transpose(1, 0, 2)
    slot = ((row_members >> 7) & 3) * 1024 + (row_members >> 9) * LANES
    slot = slot + (row_members & (LANES - 1))
    live = jnp.arange(row_members.shape[1], dtype=jnp.int32)[None, :] < row_counts[:, None]
    slot = jnp.where(live, slot, -1)
    row_chunks = jnp.clip((jnp.max(row_counts) + 15) // 16 - 1, 0, 3)
    list_chunks = jnp.clip(jnp.max(slot) // 1024, 0, 3)
    columns = anchor_cols + 1024 * (row_chunks + 4 * list_chunks)
    ordered = [
        a.reshape(2, 8, RADIX, 4, 16).transpose(3, 2, 0, 1, 4).reshape(32, LANES)
        for a in (slot, columns)
    ]
    return jnp.stack([routes.reshape(32, LANES), *ordered]).astype(jnp.int16)


def per_device(voltages, kernel, route_lists, row_members, row_counts, anchor_cols):
    chan_count = lax.axis_size("chan")
    row_count = lax.axis_size("row")
    group_size = voltages.shape[3]
    samples = voltages.shape[1]
    lists = slab_lists(route_lists, row_members, row_counts, anchor_cols)
    lists = jnp.broadcast_to(lists[None], (row_count,) + lists.shape)
    lists = lax.all_to_all(lists, "row", split_axis=0, concat_axis=0, tiled=True)
    mine = lax.dynamic_index_in_dim(voltages, lax.axis_index("row"), 1, keepdims=False)
    mine = mine.reshape(chan_count, 2, group_size // LANES, LANES)
    volts = lax.all_to_all(mine, "chan", split_axis=0, concat_axis=0, tiled=True)
    wide, tall = stage_tables()
    power = sample_power(kernel[0], volts, lists, jnp.asarray(wide), jnp.asarray(tall))
    power = power.reshape(row_count, NGRID // row_count, NGRID)
    power = lax.all_to_all(power, "row", split_axis=0, concat_axis=0, tiled=True)
    scale_factor = 1.0 / (group_size * chan_count * samples * KERNEL_SIDE * KERNEL_SIDE)
    sky_image = jnp.sum(power.astype(F32), axis=0) * scale_factor
    return sky_image.T[None]


def solution(mesh):
    in_specs = (
        P(None, None, None, "chan"),
        P("chan", None, None),
        P(None, "row", None),
        P("row", None),
        P("row"),
        P("row", None),
    )
    out_specs = P("chan", None, "row")
    return jax.shard_map(
        per_device, mesh=mesh, in_specs=in_specs, out_specs=out_specs, check_vma=False
    )
```

```python
import jax
import jax.numpy as jnp
import numpy as np
from jax import lax
from jax.experimental import pallas as pl
from jax.experimental.pallas import tpu as pltpu
from jax.sharding import PartitionSpec as P

NGRID = 1024
KERNEL_SIDE = 4
RADIX = 4
POINTS = NGRID // RADIX
LANES = 128
F32 = jnp.float32
BF16 = jnp.bfloat16


def stage_tables():
    n = np.arange(NGRID, dtype=np.int64)
    product = (n[:, None] * n[None, :POINTS]) % NGRID
    angles = product.astype(np.float32) * np.float32(-2.0 * np.pi / NGRID)
    cos = np.cos(angles).astype(np.float32)
    sin = np.sin(angles).astype(np.float32)
    parts = []
    for q in range(RADIX):
        c, s = cos[q::RADIX], sin[q::RADIX]
        parts.append(np.block([[c, s], [-s, c]]))
    table = np.stack(parts)
    return (
        np.ascontiguousarray(table.transpose(0, 2, 1)).astype(jnp.bfloat16),
        table.astype(jnp.bfloat16),
    )


def butterfly(re, im):
    ra, rb = re[0] + re[2], re[0] - re[2]
    rc, rd = re[1] + re[3], re[1] - re[3]
    ia, ib = im[0] + im[2], im[0] - im[2]
    ic, id_ = im[1] + im[3], im[1] - im[3]
    return (ra + rc, rb + id_, ra - rc, rb - id_), (ia + ic, ib - rd, ia - ic, ib + rd)


def pick(table_rows, index):
    return jnp.take_along_axis(table_rows, index, axis=1, mode="promise_in_bounds")


def sample_kernel(
    taps, volts, lists, wide, tall, power, slots, dense, aperture, spectrum,
    extent,
):
    slabs = lists.shape[0]
    groups = volts.shape[0]
    slab_points = POINTS // slabs

    for i in range(2):
        for qy in range(RADIX):
            for qx in range(RADIX):
                for w in range(2):
                    dense[i, qy, qx, w, 0:8, :] = jnp.zeros((8, LANES), F32)

    sub = lax.broadcasted_iota(jnp.int32, (8, LANES), 0)
    lane = lax.broadcasted_iota(jnp.int32, (8, LANES), 1)
    own_row = sub == lane >> 4

    for r in range(slabs):
        extent[r] = lists[r, 2].astype(jnp.int32)[0, 0] >> 10

    row_of = lax.broadcasted_iota(jnp.int32, (32, 2 * LANES), 0)
    lane_of = lax.broadcasted_iota(jnp.int32, (LANES, 2 * LANES), 0).astype(BF16)

    def gather_pair(pair, carry):
        first, second = 2 * pair, 2 * pair + 1
        routes = [lists[r, 0].astype(jnp.int32) for r in (first, second)]
        last = jnp.maximum(extent[first] & 3, extent[second] & 3)
        for s in range(4):

            @pl.when(last >= s)
            def _():
                for g in range(groups):
                    k = 8 * s + g
                    route = jnp.concatenate([a[k : k + 1, :] for a in routes], axis=1)
                    lane_spot = (route & (LANES - 1)).astype(F32).astype(BF16)
                    onehot = jnp.where(lane_of == lane_spot, BF16(1), BF16(0))
                    rows = jnp.dot(
                        volts[g].reshape(64, LANES),
                        onehot,
                        preferred_element_type=F32,
                    )
                    hit = row_of == (route >> 7)
                    for i in range(2):
                        entry = jnp.sum(
                            jnp.where(hit, rows[32 * i : 32 * i + 32], 0.0),
                            axis=0,
                            keepdims=True,
                        )
                        slots[i, first, k : k + 1, :] = entry[:, :LANES]
                        slots[i, second, k : k + 1, :] = entry[:, LANES:]

        return carry

    lax.fori_loop(0, slabs // 2, gather_pair, 0)

    def grid_chunks(r, chunks, list_rows):
        size = 8 * chunks
        members = lists[r, 1].astype(jnp.int32)[:size]
        columns = lists[r, 2].astype(jnp.int32)[:size] & (NGRID - 1)
        member_lane = members & (LANES - 1)
        member_row = members >> 7
        values = [jnp.zeros((size, LANES), F32)] * 2
        for k in range(list_rows):
            hit = member_row == k
            for i in range(2):
                row = jnp.broadcast_to(slots[i, r, k : k + 1, :], (size, LANES))
                values[i] = jnp.where(hit, pick(row, member_lane), values[i])
        kind = (columns & (RADIX - 1)) + RADIX * (columns >> 9)
        point = ((columns >> 2) & (LANES - 1)).astype(F32)
        planes = [
            jnp.where(kind == half * RADIX + qx, values[i], 0.0)
            for half in range(2)
            for qx in range(RADIX)
            for i in range(2)
        ]
        cell = lax.broadcasted_iota(jnp.int32, (LANES, chunks * LANES), 0).astype(BF16)
        for qy in range(RADIX):
            for h in range(2):
                at = [8 * c + 2 * qy + h for c in range(chunks)]
                left = jnp.concatenate(
                    [
                        jnp.concatenate(
                            [
                                jnp.where(
                                    own_row,
                                    jnp.broadcast_to(plane[a : a + 1, :], (8, LANES)),
                                    0.0,
                                )
                                for a in at
                            ],
                            axis=1,
                        )
                        for plane in planes
                    ],
                    axis=0,
                ).astype(BF16)
                spot = jnp.concatenate([point[a : a + 1, :] for a in at], axis=1)
                onehot = jnp.where(cell == spot.astype(BF16), BF16(1), BF16(0))
                placed = lax.dot_general(
                    left, onehot, (((1,), (1,)), ((), ())), preferred_element_type=F32
                )
                start = pl.multiple_of(8 + r * slab_points + 8 * h, 8)
                for half in range(2):
                    for qx in range(RADIX):
                        for i in range(2):
                            a = ((half * RADIX + qx) * 2 + i) * 8
                            dense[i, qy, qx, half, pl.ds(start, 8), :] = placed[
                                a : a + 8, :
                            ]

    def grid_slab(r, carry):
        @pl.when(extent[r] < 4)
        def _():
            grid_chunks(r, 2, 16)

        @pl.when(extent[r] >= 4)
        def _():
            grid_chunks(r, 4, 32)

        return carry

    lax.fori_loop(0, slabs, grid_slab, 0)

    first_lane = lax.broadcasted_iota(jnp.int32, (16, POINTS), 1) == 0

    def convolve(t, carry):
        for i in range(2):
            for qy in range(RADIX):
                sums = [jnp.zeros((16, POINTS), F32) for _ in range(RADIX)]
                for ky in range(KERNEL_SIDE):
                    source = (qy - ky) % RADIX
                    start = 8 + 16 * t - (1 if ky > qy else 0)
                    here = [
                        jnp.concatenate(
                            [
                                dense[i, source, qx, w, pl.ds(start, 16), :]
                                for w in range(2)
                            ],
                            axis=1,
                        )
                        for qx in range(RADIX)
                    ]
                    before = [
                        None
                        if qx == 0
                        else jnp.where(first_lane, 0.0, pltpu.roll(here[qx], 1, 1))
                        for qx in range(RADIX)
                    ]
                    for qx in range(RADIX):
                        for kx in range(KERNEL_SIDE):
                            near = before if kx > qx else here
                            sums[qx] = (
                                sums[qx] + taps[ky, kx] * near[(qx - kx) % RADIX]
                            )
                row = pl.multiple_of(qy * POINTS + 16 * t, 16)
                for qx in range(RADIX):
                    at = (2 * qx + i) * POINTS
                    aperture[pl.ds(row, 16), at : at + POINTS] = sums[qx].astype(BF16)
        return carry

    lax.fori_loop(0, POINTS // 16, convolve, 0)

    def row_transform(qy, carry):
        rows = pl.ds(pl.multiple_of(qy * POINTS, POINTS), POINTS)
        parts = [
            lax.dot_general(
                wide[q],
                aperture[rows, 2 * q * POINTS : 2 * (q + 1) * POINTS],
                (((1,), (1,)), ((), ())),
                preferred_element_type=F32,
            )
            for q in range(RADIX)
        ]
        re, im = butterfly(
            [part[:POINTS] for part in parts], [part[POINTS:] for part in parts]
        )
        at = pl.multiple_of(qy * 2 * POINTS, 2 * POINTS)
        for m in range(RADIX):
            spectrum[m * POINTS : (m + 1) * POINTS, pl.ds(at, POINTS)] = re[m].astype(
                BF16
            )
            spectrum[
                m * POINTS : (m + 1) * POINTS, pl.ds(at + POINTS, POINTS)
            ] = im[m].astype(BF16)
        return carry

    lax.fori_loop(0, RADIX, row_transform, 0)

    def column_transform(n, carry):
        rows = pl.ds(pl.multiple_of(n * 256, 256), 256)
        parts = [
            jnp.dot(
                spectrum[rows, 2 * q * POINTS : 2 * (q + 1) * POINTS],
                tall[q],
                preferred_element_type=F32,
            )
            for q in range(RADIX)
        ]
        re, im = butterfly(
            [part[:, :POINTS] for part in parts], [part[:, POINTS:] for part in parts]
        )
        for m in range(RADIX):
            power[rows, m * POINTS : (m + 1) * POINTS] = (
                re[m] * re[m] + im[m] * im[m]
            ).astype(BF16)
        return carry

    lax.fori_loop(0, NGRID // 256, column_transform, 0)


def sample_power(taps, volts, lists, wide, tall, interpret=False):
    return pl.pallas_call(
        sample_kernel,
        out_shape=jax.ShapeDtypeStruct((NGRID, NGRID), BF16),
        in_specs=[pl.BlockSpec(memory_space=pltpu.SMEM)]
        + [pl.BlockSpec(memory_space=pltpu.VMEM)] * 4,
        out_specs=pl.BlockSpec(memory_space=pltpu.VMEM),
        scratch_shapes=[
            pltpu.VMEM((2, lists.shape[0], 32, LANES), F32),
            pltpu.VMEM((2, RADIX, RADIX, 2, POINTS + 8, LANES), F32),
            pltpu.VMEM((NGRID, 2 * NGRID), BF16),
            pltpu.VMEM((NGRID, 2 * NGRID), BF16),
            pltpu.SMEM((lists.shape[0],), jnp.int32),
        ],
        compiler_params=pltpu.CompilerParams(vmem_limit_bytes=40 * 2**20),
        interpret=interpret,
    )(taps, volts, lists, wide, tall)


def slab_lists(route_lists, row_members, row_counts, anchor_cols):
    routes = route_lists[:, 0, :].reshape(8, 4, LANES).transpose(1, 0, 2)
    slot = ((row_members >> 7) & 3) * 1024 + (row_members >> 9) * LANES
    slot = slot + (row_members & (LANES - 1))
    live = jnp.arange(row_members.shape[1], dtype=jnp.int32)[None, :] < row_counts[:, None]
    slot = jnp.where(live, slot, -1)
    top = jnp.max(slot)
    wide = (jnp.max(row_counts) > 32) | (top >= 2048)
    extent = (jnp.maximum(top, 0) >> 10) + jnp.where(wide, 4, 0)
    columns = anchor_cols + 1024 * extent
    ordered = [
        a.reshape(2, 8, RADIX, 4, 16).transpose(3, 2, 0, 1, 4).reshape(32, LANES)
        for a in (slot, columns)
    ]
    return jnp.stack([routes.reshape(32, LANES), *ordered]).astype(jnp.int16)


def per_device(voltages, kernel, route_lists, row_members, row_counts, anchor_cols):
    chan_count = lax.axis_size("chan")
    row_count = lax.axis_size("row")
    group_size = voltages.shape[3]
    samples = voltages.shape[1]
    lists = slab_lists(route_lists, row_members, row_counts, anchor_cols)
    lists = jnp.broadcast_to(lists[None], (row_count,) + lists.shape)
    lists = lax.all_to_all(lists, "row", split_axis=0, concat_axis=0, tiled=True)
    mine = lax.dynamic_index_in_dim(voltages, lax.axis_index("row"), 1, keepdims=False)
    mine = mine.reshape(chan_count, 2, group_size // LANES, LANES)
    volts = lax.all_to_all(mine, "chan", split_axis=0, concat_axis=0, tiled=True)
    wide, tall = stage_tables()
    power = sample_power(kernel[0], volts, lists, jnp.asarray(wide), jnp.asarray(tall))
    power = power.reshape(row_count, NGRID // row_count, NGRID)
    power = lax.all_to_all(power, "row", split_axis=0, concat_axis=0, tiled=True)
    scale_factor = 1.0 / (group_size * chan_count * samples * KERNEL_SIDE * KERNEL_SIDE)
    sky_image = jnp.sum(power.astype(F32), axis=0) * scale_factor
    return sky_image.T[None]


def solution(mesh):
    in_specs = (
        P(None, None, None, "chan"),
        P("chan", None, None),
        P(None, "row", None),
        P("row", None),
        P("row"),
        P("row", None),
    )
    out_specs = P("chan", None, "row")
    return jax.shard_map(
        per_device, mesh=mesh, in_specs=in_specs, out_specs=out_specs, check_vma=False
    )
```

```python
import jax
import jax.numpy as jnp
import numpy as np
from jax import lax
from jax.experimental import pallas as pl
from jax.experimental.pallas import tpu as pltpu
from jax.sharding import PartitionSpec as P

NGRID = 1024
KERNEL_SIDE = 4
RADIX = 4
POINTS = NGRID // RADIX
LANES = 128
F32 = jnp.float32
BF16 = jnp.bfloat16


def stage_tables():
    n = np.arange(NGRID, dtype=np.int64)
    product = (n[:, None] * n[None, :POINTS]) % NGRID
    angles = product.astype(np.float32) * np.float32(-2.0 * np.pi / NGRID)
    cos = np.cos(angles).astype(np.float32)
    sin = np.sin(angles).astype(np.float32)
    parts = []
    for q in range(RADIX):
        c, s = cos[q::RADIX], sin[q::RADIX]
        parts.append(np.block([[c, s], [-s, c]]))
    table = np.stack(parts)
    return (
        np.ascontiguousarray(table.transpose(0, 2, 1)).astype(jnp.bfloat16),
        table.astype(jnp.bfloat16),
    )


def butterfly(re, im):
    ra, rb = re[0] + re[2], re[0] - re[2]
    rc, rd = re[1] + re[3], re[1] - re[3]
    ia, ib = im[0] + im[2], im[0] - im[2]
    ic, id_ = im[1] + im[3], im[1] - im[3]
    return (ra + rc, rb + id_, ra - rc, rb - id_), (ia + ic, ib - rd, ia - ic, ib + rd)


def pick(table_rows, index):
    return jnp.take_along_axis(table_rows, index, axis=1, mode="promise_in_bounds")


def sample_kernel(
    taps, extent, volts, lists, wide_from, tall_from, power, slots, dense, aperture,
    spectrum, wide, tall, arrived,
):
    slabs = lists.shape[0]
    groups = volts.shape[0]
    slab_points = POINTS // slabs
    wide_copy = pltpu.make_async_copy(wide_from, wide, arrived.at[0])
    tall_copy = pltpu.make_async_copy(tall_from, tall, arrived.at[1])
    wide_copy.start()
    tall_copy.start()

    for i in range(2):
        for qy in range(RADIX):
            for qx in range(RADIX):
                for w in range(2):
                    dense[i, qy, qx, w, 0:8, :] = jnp.zeros((8, LANES), F32)

    sub = lax.broadcasted_iota(jnp.int32, (8, LANES), 0)
    lane = lax.broadcasted_iota(jnp.int32, (8, LANES), 1)
    own_row = sub == lane >> 4

    row_of = lax.broadcasted_iota(jnp.int32, (32, 2 * LANES), 0)
    lane_of = lax.broadcasted_iota(jnp.int32, (LANES, 2 * LANES), 0).astype(BF16)

    def gather_pair(pair, carry):
        first, second = 2 * pair, 2 * pair + 1
        routes = [lists[r, 0].astype(jnp.int32) for r in (first, second)]
        last = jnp.maximum(extent[first] & 3, extent[second] & 3)
        for s in range(4):

            @pl.when(last >= s)
            def _():
                for g in range(groups):
                    k = 8 * s + g
                    route = jnp.concatenate([a[k : k + 1, :] for a in routes], axis=1)
                    lane_spot = (route & (LANES - 1)).astype(F32).astype(BF16)
                    onehot = jnp.where(lane_of == lane_spot, BF16(1), BF16(0))
                    rows = jnp.dot(
                        volts[g].reshape(64, LANES),
                        onehot,
                        preferred_element_type=F32,
                    )
                    hit = row_of == (route >> 7)
                    for i in range(2):
                        entry = jnp.sum(
                            jnp.where(hit, rows[32 * i : 32 * i + 32], 0.0),
                            axis=0,
                            keepdims=True,
                        )
                        slots[i, first, k : k + 1, :] = entry[:, :LANES]
                        slots[i, second, k : k + 1, :] = entry[:, LANES:]

        return carry

    lax.fori_loop(0, slabs // 2, gather_pair, 0)

    def grid_chunks(r, chunks, list_rows):
        size = 8 * chunks
        members = lists[r, 1].astype(jnp.int32)[:size]
        columns = lists[r, 2].astype(jnp.int32)[:size]
        member_lane = members & (LANES - 1)
        member_row = members >> 7
        values = [jnp.zeros((size, LANES), F32)] * 2
        for k in range(list_rows):
            hit = member_row == k
            for i in range(2):
                row = jnp.broadcast_to(slots[i, r, k : k + 1, :], (size, LANES))
                values[i] = jnp.where(hit, pick(row, member_lane), values[i])
        kind = (columns & (RADIX - 1)) + RADIX * (columns >> 9)
        point = ((columns >> 2) & (LANES - 1)).astype(F32)
        planes = [
            jnp.where(kind == half * RADIX + qx, values[i], 0.0)
            for half in range(2)
            for qx in range(RADIX)
            for i in range(2)
        ]
        cell = lax.broadcasted_iota(jnp.int32, (LANES, chunks * LANES), 0).astype(BF16)
        for qy in range(RADIX):
            for h in range(2):
                at = [8 * c + 2 * qy + h for c in range(chunks)]
                left = jnp.concatenate(
                    [
                        jnp.concatenate(
                            [
                                jnp.where(
                                    own_row,
                                    jnp.broadcast_to(plane[a : a + 1, :], (8, LANES)),
                                    0.0,
                                )
                                for a in at
                            ],
                            axis=1,
                        )
                        for plane in planes
                    ],
                    axis=0,
                ).astype(BF16)
                spot = jnp.concatenate([point[a : a + 1, :] for a in at], axis=1)
                onehot = jnp.where(cell == spot.astype(BF16), BF16(1), BF16(0))
                placed = lax.dot_general(
                    left, onehot, (((1,), (1,)), ((), ())), preferred_element_type=F32
                )
                start = pl.multiple_of(8 + r * slab_points + 8 * h, 8)
                for half in range(2):
                    for qx in range(RADIX):
                        for i in range(2):
                            a = ((half * RADIX + qx) * 2 + i) * 8
                            dense[i, qy, qx, half, pl.ds(start, 8), :] = placed[
                                a : a + 8, :
                            ]

    def grid_slab(r, carry):
        @pl.when(extent[r] < 4)
        def _():
            grid_chunks(r, 2, 16)

        @pl.when(extent[r] >= 4)
        def _():
            grid_chunks(r, 4, 32)

        return carry

    lax.fori_loop(0, slabs, grid_slab, 0)

    first_lane = lax.broadcasted_iota(jnp.int32, (16, POINTS), 1) == 0

    def convolve(t, carry):
        for i in range(2):
            for qy in range(RADIX):
                sums = [jnp.zeros((16, POINTS), F32) for _ in range(RADIX)]
                for ky in range(KERNEL_SIDE):
                    source = (qy - ky) % RADIX
                    start = 8 + 16 * t - (1 if ky > qy else 0)
                    here = [
                        jnp.concatenate(
                            [
                                dense[i, source, qx, w, pl.ds(start, 16), :]
                                for w in range(2)
                            ],
                            axis=1,
                        )
                        for qx in range(RADIX)
                    ]
                    before = [
                        None
                        if qx == 0
                        else jnp.where(first_lane, 0.0, pltpu.roll(here[qx], 1, 1))
                        for qx in range(RADIX)
                    ]
                    for qx in range(RADIX):
                        for kx in range(KERNEL_SIDE):
                            near = before if kx > qx else here
                            sums[qx] = (
                                sums[qx] + taps[ky, kx] * near[(qx - kx) % RADIX]
                            )
                row = pl.multiple_of(qy * POINTS + 16 * t, 16)
                for qx in range(RADIX):
                    at = (2 * qx + i) * POINTS
                    aperture[pl.ds(row, 16), at : at + POINTS] = sums[qx].astype(BF16)
        return carry

    lax.fori_loop(0, POINTS // 16, convolve, 0)

    def row_transform(qy, carry):
        rows = pl.ds(pl.multiple_of(qy * POINTS, POINTS), POINTS)
        parts = [
            lax.dot_general(
                wide[q],
                aperture[rows, 2 * q * POINTS : 2 * (q + 1) * POINTS],
                (((1,), (1,)), ((), ())),
                preferred_element_type=F32,
            )
            for q in range(RADIX)
        ]
        re, im = butterfly(
            [part[:POINTS] for part in parts], [part[POINTS:] for part in parts]
        )
        at = pl.multiple_of(qy * 2 * POINTS, 2 * POINTS)
        for m in range(RADIX):
            spectrum[m * POINTS : (m + 1) * POINTS, pl.ds(at, POINTS)] = re[m].astype(
                BF16
            )
            spectrum[
                m * POINTS : (m + 1) * POINTS, pl.ds(at + POINTS, POINTS)
            ] = im[m].astype(BF16)
        return carry

    wide_copy.wait()
    lax.fori_loop(0, RADIX, row_transform, 0)

    def column_transform(n, carry):
        rows = pl.ds(pl.multiple_of(n * 256, 256), 256)
        parts = [
            jnp.dot(
                spectrum[rows, 2 * q * POINTS : 2 * (q + 1) * POINTS],
                tall[q],
                preferred_element_type=F32,
            )
            for q in range(RADIX)
        ]
        re, im = butterfly(
            [part[:, :POINTS] for part in parts], [part[:, POINTS:] for part in parts]
        )
        for m in range(RADIX):
            power[rows, m * POINTS : (m + 1) * POINTS] = (
                re[m] * re[m] + im[m] * im[m]
            ).astype(BF16)
        return carry

    tall_copy.wait()
    lax.fori_loop(0, NGRID // 256, column_transform, 0)


def sample_power(taps, extent, volts, lists, wide, tall):
    return pl.pallas_call(
        sample_kernel,
        out_shape=jax.ShapeDtypeStruct((NGRID, NGRID), BF16),
        in_specs=[pl.BlockSpec(memory_space=pltpu.SMEM)] * 2
        + [pl.BlockSpec(memory_space=pltpu.VMEM)] * 2
        + [pl.BlockSpec(memory_space=pl.ANY)] * 2,
        out_specs=pl.BlockSpec(memory_space=pltpu.VMEM),
        scratch_shapes=[
            pltpu.VMEM((2, lists.shape[0], 32, LANES), F32),
            pltpu.VMEM((2, RADIX, RADIX, 2, POINTS + 8, LANES), F32),
            pltpu.VMEM((NGRID, 2 * NGRID), BF16),
            pltpu.VMEM((NGRID, 2 * NGRID), BF16),
            pltpu.VMEM(wide.shape, BF16),
            pltpu.VMEM(tall.shape, BF16),
            pltpu.SemaphoreType.DMA((2,)),
        ],
        compiler_params=pltpu.CompilerParams(vmem_limit_bytes=56 * 2**20),
    )(taps, extent, volts, lists, wide, tall)


def slab_lists(route_lists, row_members, row_counts, anchor_cols):
    routes = route_lists[:, 0, :].reshape(8, 4, LANES).transpose(1, 0, 2)
    slot = ((row_members >> 7) & 3) * 1024 + (row_members >> 9) * LANES
    slot = slot + (row_members & (LANES - 1))
    live = jnp.arange(row_members.shape[1], dtype=jnp.int32)[None, :] < row_counts[:, None]
    slot = jnp.where(live, slot, -1)
    ordered = [
        a.reshape(2, 8, RADIX, 4, 16).transpose(3, 2, 0, 1, 4).reshape(32, LANES)
        for a in (slot, anchor_cols)
    ]
    return jnp.stack([routes.reshape(32, LANES), *ordered]).astype(jnp.int16)


def list_extents(lists):
    slot = lists[:, 1].astype(jnp.int32)
    top = jnp.max(slot, axis=(1, 2))
    late = jnp.max(slot[:, 16:], axis=(1, 2))
    wide = (top >= 2048) | (late >= 0)
    return (jnp.maximum(top, 0) >> 10) + jnp.where(wide, 4, 0)


def per_device(voltages, kernel, route_lists, row_members, row_counts, anchor_cols):
    chan_count = lax.axis_size("chan")
    row_count = lax.axis_size("row")
    group_size = voltages.shape[3]
    samples = voltages.shape[1]
    lists = slab_lists(route_lists, row_members, row_counts, anchor_cols)
    lists = jnp.broadcast_to(lists[None], (row_count,) + lists.shape)
    lists = lax.all_to_all(lists, "row", split_axis=0, concat_axis=0, tiled=True)
    mine = lax.dynamic_index_in_dim(voltages, lax.axis_index("row"), 1, keepdims=False)
    mine = mine.reshape(chan_count, 2, group_size // LANES, LANES)
    lists, mine = lax.optimization_barrier((lists, mine))
    volts = lax.all_to_all(mine, "chan", split_axis=0, concat_axis=0, tiled=True)
    wide, tall = stage_tables()
    power = sample_power(
        kernel[0],
        list_extents(lists),
        volts,
        lists,
        jnp.asarray(wide),
        jnp.asarray(tall),
    )
    power = power.reshape(row_count, NGRID // row_count, NGRID)
    power = lax.all_to_all(power, "row", split_axis=0, concat_axis=0, tiled=True)
    scale_factor = 1.0 / (group_size * chan_count * samples * KERNEL_SIDE * KERNEL_SIDE)
    sky_image = jnp.sum(power.astype(F32), axis=0) * scale_factor
    return sky_image.T[None]


def solution(mesh):
    in_specs = (
        P(None, None, None, "chan"),
        P("chan", None, None),
        P(None, "row", None),
        P("row", None),
        P("row"),
        P("row", None),
    )
    out_specs = P("chan", None, "row")
    return jax.shard_map(
        per_device, mesh=mesh, in_specs=in_specs, out_specs=out_specs, check_vma=False
    )
```

```python
import jax
import jax.numpy as jnp
import numpy as np
from jax import lax
from jax.experimental import pallas as pl
from jax.experimental.pallas import tpu as pltpu
from jax.sharding import PartitionSpec as P

NGRID = 1024
KERNEL_SIDE = 4
SLAB = 64
RADIX = 4
POINTS = NGRID // RADIX
LANES = 128
F32 = jnp.float32
BF16 = jnp.bfloat16


def stage_tables():
    n = np.arange(NGRID, dtype=np.int64)
    product = (n[:, None] * n[None, :POINTS]) % NGRID
    angles = product.astype(np.float32) * np.float32(-2.0 * np.pi / NGRID)
    cos = np.cos(angles).astype(np.float32)
    sin = np.sin(angles).astype(np.float32)
    parts = []
    for q in range(RADIX):
        c, s = cos[q::RADIX], sin[q::RADIX]
        parts.append(np.block([[c, s], [-s, c]]))
    table = np.stack(parts)
    return (
        np.ascontiguousarray(table.transpose(0, 2, 1)).astype(jnp.bfloat16),
        table.astype(jnp.bfloat16),
    )


def butterfly(re, im):
    ra, rb = re[0] + re[2], re[0] - re[2]
    rc, rd = re[1] + re[3], re[1] - re[3]
    ia, ib = im[0] + im[2], im[0] - im[2]
    ic, id_ = im[1] + im[3], im[1] - im[3]
    return (ra + rc, rb + id_, ra - rc, rb - id_), (ia + ic, ib - rd, ia - ic, ib + rd)


def pick(table_rows, index):
    return jnp.take_along_axis(table_rows, index, axis=1, mode="promise_in_bounds")


def sample_kernel(
    taps, extent, volts, lists, wide_from, tall_from, power, slots, bands, cells, aperture,
    spectrum, wide, tall, arrived,
):
    slabs = lists.shape[0]
    groups = volts.shape[0]
    slab_points = POINTS // slabs
    wide_copy = pltpu.make_async_copy(wide_from, wide, arrived.at[0])
    tall_copy = pltpu.make_async_copy(tall_from, tall, arrived.at[1])
    wide_copy.start()
    tall_copy.start()

    down = lax.broadcasted_iota(jnp.int32, (SLAB, 4 * SLAB), 0)
    across = lax.broadcasted_iota(jnp.int32, (SLAB, 4 * SLAB), 1)
    apart = RADIX * (down & 15) + (down >> 4)
    apart = apart - RADIX * (across & 15) - ((across >> 4) & 3)
    apart = apart + SLAB * ((across >> 6) & 1)
    for kx in range(KERNEL_SIDE):
        tap = jnp.zeros((SLAB, 4 * SLAB), F32)
        for ky in range(KERNEL_SIDE):
            tap = jnp.where(apart == ky, taps[ky, kx], tap)
        high = tap.astype(BF16).astype(F32)
        bands[kx * SLAB : (kx + 1) * SLAB, :] = jnp.where(
            across < 2 * SLAB, high, tap - high
        ).astype(BF16)
    cells[2] = jnp.zeros(cells.shape[1:], BF16)

    sub = lax.broadcasted_iota(jnp.int32, (8, LANES), 0)
    lane = lax.broadcasted_iota(jnp.int32, (8, LANES), 1)
    own_row = sub == lane >> 4
    first_lane = lax.broadcasted_iota(jnp.int32, (SLAB, POINTS), 1) == 0

    row_of = lax.broadcasted_iota(jnp.int32, (32, 2 * LANES), 0)
    lane_of = lax.broadcasted_iota(jnp.int32, (LANES, 2 * LANES), 0).astype(BF16)

    def gather_pair(pair, carry):
        first, second = 2 * pair, 2 * pair + 1
        routes = [lists[r, 0].astype(jnp.int32) for r in (first, second)]
        last = jnp.maximum(extent[first] & 3, extent[second] & 3)
        for s in range(4):

            @pl.when(last >= s)
            def _():
                for g in range(groups):
                    k = 8 * s + g
                    route = jnp.concatenate([a[k : k + 1, :] for a in routes], axis=1)
                    lane_spot = (route & (LANES - 1)).astype(F32).astype(BF16)
                    onehot = jnp.where(lane_of == lane_spot, BF16(1), BF16(0))
                    rows = jnp.dot(
                        volts[g].reshape(64, LANES),
                        onehot,
                        preferred_element_type=F32,
                    )
                    hit = row_of == (route >> 7)
                    for i in range(2):
                        entry = jnp.sum(
                            jnp.where(hit, rows[32 * i : 32 * i + 32], 0.0),
                            axis=0,
                            keepdims=True,
                        )
                        slots[i, first, k : k + 1, :] = entry[:, :LANES]
                        slots[i, second, k : k + 1, :] = entry[:, LANES:]

        return carry

    lax.fori_loop(0, slabs // 2, gather_pair, 0)

    def convolve(r):
        here = lax.rem(r + 3, 3)
        before = lax.rem(r + 2, 3)
        for i in range(2):
            sums = []
            for q in range(RADIX):
                rows = [cells[here, 2 * q + i], cells[before, 2 * q + i]]
                sums.append(
                    jnp.dot(
                        bands[...],
                        jnp.concatenate(rows + rows, axis=0),
                        preferred_element_type=F32,
                    )
                )
            for qx in range(RADIX):
                terms = [
                    sums[(qx - kx) % RADIX][kx * SLAB : (kx + 1) * SLAB]
                    for kx in range(KERNEL_SIDE)
                ]
                total = sum(terms[1 : qx + 1], terms[0])
                if qx < KERNEL_SIDE - 1:
                    spill = sum(terms[qx + 2 :], terms[qx + 1])
                    spill = pltpu.roll(spill, 1, 1)
                    total = total + jnp.where(first_lane, 0.0, spill)
                total = total.astype(BF16)
                at = (2 * qx + i) * POINTS
                for qy in range(RADIX):
                    row = pl.multiple_of(qy * POINTS + slab_points * jnp.maximum(r, 0), 16)
                    aperture[pl.ds(row, 16), at : at + POINTS] = total[
                        16 * qy : 16 * qy + 16
                    ]

    def grid_chunks(r, chunks, list_rows):
        convolve(r - 1)
        place = lax.rem(r, 3)
        size = 8 * chunks
        members = lists[r, 1].astype(jnp.int32)[:size]
        columns = lists[r, 2].astype(jnp.int32)[:size]
        member_lane = members & (LANES - 1)
        member_row = members >> 7
        values = [jnp.zeros((size, LANES), F32)] * 2
        for k in range(list_rows):
            hit = member_row == k
            for i in range(2):
                row = jnp.broadcast_to(slots[i, r, k : k + 1, :], (size, LANES))
                values[i] = jnp.where(hit, pick(row, member_lane), values[i])
        kind = (columns & (RADIX - 1)) + RADIX * (columns >> 9)
        point = ((columns >> 2) & (LANES - 1)).astype(F32)
        planes = [
            jnp.where(kind == half * RADIX + qx, values[i], 0.0)
            for half in range(2)
            for qx in range(RADIX)
            for i in range(2)
        ]
        cell = lax.broadcasted_iota(jnp.int32, (LANES, chunks * LANES), 0).astype(BF16)
        for qy in range(RADIX):
            placed = []
            for h in range(2):
                at = [8 * c + 2 * qy + h for c in range(chunks)]
                left = jnp.concatenate(
                    [
                        jnp.concatenate(
                            [
                                jnp.where(
                                    own_row,
                                    jnp.broadcast_to(plane[a : a + 1, :], (8, LANES)),
                                    0.0,
                                )
                                for a in at
                            ],
                            axis=1,
                        )
                        for plane in planes
                    ],
                    axis=0,
                ).astype(BF16)
                spot = jnp.concatenate([point[a : a + 1, :] for a in at], axis=1)
                onehot = jnp.where(cell == spot.astype(BF16), BF16(1), BF16(0))
                placed.append(
                    lax.dot_general(
                        left,
                        onehot,
                        (((1,), (1,)), ((), ())),
                        preferred_element_type=F32,
                    )
                )
            for half in range(2):
                for plane in range(2 * RADIX):
                    a = (half * 2 * RADIX + plane) * 8
                    cells[
                        place,
                        plane,
                        16 * qy : 16 * qy + 16,
                        half * LANES : (half + 1) * LANES,
                    ] = jnp.concatenate([p[a : a + 8, :] for p in placed], axis=0).astype(
                        BF16
                    )

    def grid_slab(r, carry):
        @pl.when(extent[r] < 4)
        def _():
            grid_chunks(r, 2, 16)

        @pl.when(extent[r] >= 4)
        def _():
            grid_chunks(r, 4, 32)

        return carry

    lax.fori_loop(0, slabs, grid_slab, 0)
    convolve(slabs - 1)

    def row_transform(qy, carry):
        rows = pl.ds(pl.multiple_of(qy * POINTS, POINTS), POINTS)
        parts = [
            lax.dot_general(
                wide[q],
                aperture[rows, 2 * q * POINTS : 2 * (q + 1) * POINTS],
                (((1,), (1,)), ((), ())),
                preferred_element_type=F32,
            )
            for q in range(RADIX)
        ]
        re, im = butterfly(
            [part[:POINTS] for part in parts], [part[POINTS:] for part in parts]
        )
        at = pl.multiple_of(qy * 2 * POINTS, 2 * POINTS)
        for m in range(RADIX):
            spectrum[m * POINTS : (m + 1) * POINTS, pl.ds(at, POINTS)] = re[m].astype(
                BF16
            )
            spectrum[
                m * POINTS : (m + 1) * POINTS, pl.ds(at + POINTS, POINTS)
            ] = im[m].astype(BF16)
        return carry

    wide_copy.wait()
    lax.fori_loop(0, RADIX, row_transform, 0)

    def column_transform(n, carry):
        rows = pl.ds(pl.multiple_of(n * 256, 256), 256)
        parts = [
            jnp.dot(
                spectrum[rows, 2 * q * POINTS : 2 * (q + 1) * POINTS],
                tall[q],
                preferred_element_type=F32,
            )
            for q in range(RADIX)
        ]
        re, im = butterfly(
            [part[:, :POINTS] for part in parts], [part[:, POINTS:] for part in parts]
        )
        for m in range(RADIX):
            power[rows, m * POINTS : (m + 1) * POINTS] = (
                re[m] * re[m] + im[m] * im[m]
            ).astype(BF16)
        return carry

    tall_copy.wait()
    lax.fori_loop(0, NGRID // 256, column_transform, 0)


def sample_power(taps, extent, volts, lists, wide, tall):
    return pl.pallas_call(
        sample_kernel,
        out_shape=jax.ShapeDtypeStruct((NGRID, NGRID), BF16),
        in_specs=[pl.BlockSpec(memory_space=pltpu.SMEM)] * 2
        + [pl.BlockSpec(memory_space=pltpu.VMEM)] * 2
        + [pl.BlockSpec(memory_space=pl.ANY)] * 2,
        out_specs=pl.BlockSpec(memory_space=pltpu.VMEM),
        scratch_shapes=[
            pltpu.VMEM((2, lists.shape[0], 32, LANES), F32),
            pltpu.VMEM((4 * SLAB, 4 * SLAB), BF16),
            pltpu.VMEM((3, 2 * RADIX, SLAB, POINTS), BF16),
            pltpu.VMEM((NGRID, 2 * NGRID), BF16),
            pltpu.VMEM((NGRID, 2 * NGRID), BF16),
            pltpu.VMEM(wide.shape, BF16),
            pltpu.VMEM(tall.shape, BF16),
            pltpu.SemaphoreType.DMA((2,)),
        ],
        compiler_params=pltpu.CompilerParams(vmem_limit_bytes=56 * 2**20),
    )(taps, extent, volts, lists, wide, tall)


def slab_lists(route_lists, row_members, row_counts, anchor_cols):
    routes = route_lists[:, 0, :].reshape(8, 4, LANES).transpose(1, 0, 2)
    slot = ((row_members >> 7) & 3) * 1024 + (row_members >> 9) * LANES
    slot = slot + (row_members & (LANES - 1))
    live = jnp.arange(row_members.shape[1], dtype=jnp.int32)[None, :] < row_counts[:, None]
    slot = jnp.where(live, slot, -1)
    ordered = [
        a.reshape(2, 8, RADIX, 4, 16).transpose(3, 2, 0, 1, 4).reshape(32, LANES)
        for a in (slot, anchor_cols)
    ]
    return jnp.stack([routes.reshape(32, LANES), *ordered]).astype(jnp.int16)


def list_extents(lists):
    slot = lists[:, 1].astype(jnp.int32)
    top = jnp.max(slot, axis=(1, 2))
    late = jnp.max(slot[:, 16:], axis=(1, 2))
    wide = (top >= 2048) | (late >= 0)
    return (jnp.maximum(top, 0) >> 10) + jnp.where(wide, 4, 0)


def per_device(voltages, kernel, route_lists, row_members, row_counts, anchor_cols):
    chan_count = lax.axis_size("chan")
    row_count = lax.axis_size("row")
    group_size = voltages.shape[3]
    samples = voltages.shape[1]
    lists = slab_lists(route_lists, row_members, row_counts, anchor_cols)
    lists = jnp.broadcast_to(lists[None], (row_count,) + lists.shape)
    lists = lax.all_to_all(lists, "row", split_axis=0, concat_axis=0, tiled=True)
    mine = lax.dynamic_index_in_dim(voltages, lax.axis_index("row"), 1, keepdims=False)
    mine = mine.reshape(chan_count, 2, group_size // LANES, LANES)
    lists, mine = lax.optimization_barrier((lists, mine))
    volts = lax.all_to_all(mine, "chan", split_axis=0, concat_axis=0, tiled=True)
    wide, tall = stage_tables()
    power = sample_power(
        kernel[0],
        list_extents(lists),
        volts,
        lists,
        jnp.asarray(wide),
        jnp.asarray(tall),
    )
    power = power.reshape(row_count, NGRID // row_count, NGRID)
    power = lax.all_to_all(power, "row", split_axis=0, concat_axis=0, tiled=True)
    scale_factor = 1.0 / (group_size * chan_count * samples * KERNEL_SIDE * KERNEL_SIDE)
    sky_image = jnp.sum(power.astype(F32), axis=0) * scale_factor
    return sky_image.T[None]


def solution(mesh):
    in_specs = (
        P(None, None, None, "chan"),
        P("chan", None, None),
        P(None, "row", None),
        P("row", None),
        P("row"),
        P("row", None),
    )
    out_specs = P("chan", None, "row")
    return jax.shard_map(
        per_device, mesh=mesh, in_specs=in_specs, out_specs=out_specs, check_vma=False
    )
```

```python
import jax
import jax.numpy as jnp
import numpy as np
from jax import lax
from jax.experimental import pallas as pl
from jax.experimental.pallas import tpu as pltpu
from jax.sharding import PartitionSpec as P

NGRID = 1024
KERNEL_SIDE = 4
SLAB = 64
RADIX = 4
POINTS = NGRID // RADIX
LANES = 128
F32 = jnp.float32
BF16 = jnp.bfloat16


def stage_tables():
    n = np.arange(NGRID, dtype=np.int64)
    product = (n[:, None] * n[None, :POINTS]) % NGRID
    angles = product.astype(np.float32) * np.float32(-2.0 * np.pi / NGRID)
    cos = np.cos(angles).astype(np.float32)
    sin = np.sin(angles).astype(np.float32)
    parts = []
    for q in range(RADIX):
        c, s = cos[q::RADIX], sin[q::RADIX]
        parts.append(np.block([[c, s], [-s, c]]))
    table = np.stack(parts)
    return (
        np.ascontiguousarray(table.transpose(0, 2, 1)).astype(jnp.bfloat16),
        table.astype(jnp.bfloat16),
    )


def butterfly(re, im):
    ra, rb = re[0] + re[2], re[0] - re[2]
    rc, rd = re[1] + re[3], re[1] - re[3]
    ia, ib = im[0] + im[2], im[0] - im[2]
    ic, id_ = im[1] + im[3], im[1] - im[3]
    return (ra + rc, rb + id_, ra - rc, rb - id_), (ia + ic, ib - rd, ia - ic, ib + rd)


def pick(table_rows, index):
    return jnp.take_along_axis(table_rows, index, axis=1, mode="promise_in_bounds")


def sample_kernel(
    taps, extent, volts, lists, wide_from, tall_from, power_to, slots, bands, cells, aperture,
    spectrum, wide, tall, power, arrived, left_for,
):
    slabs = lists.shape[0]
    groups = volts.shape[0]
    slab_points = POINTS // slabs
    wide_copy = pltpu.make_async_copy(wide_from, wide, arrived.at[0])
    tall_copy = pltpu.make_async_copy(tall_from, tall, arrived.at[1])
    wide_copy.start()
    tall_copy.start()

    down = lax.broadcasted_iota(jnp.int32, (SLAB, 4 * SLAB), 0)
    across = lax.broadcasted_iota(jnp.int32, (SLAB, 4 * SLAB), 1)
    apart = RADIX * (down & 15) + (down >> 4)
    apart = apart - RADIX * (across & 15) - ((across >> 4) & 3)
    apart = apart + SLAB * ((across >> 6) & 1)
    for kx in range(KERNEL_SIDE):
        tap = jnp.zeros((SLAB, 4 * SLAB), F32)
        for ky in range(KERNEL_SIDE):
            tap = jnp.where(apart == ky, taps[ky, kx], tap)
        high = tap.astype(BF16).astype(F32)
        bands[kx * SLAB : (kx + 1) * SLAB, :] = jnp.where(
            across < 2 * SLAB, high, tap - high
        ).astype(BF16)
    cells[2] = jnp.zeros(cells.shape[1:], BF16)

    sub = lax.broadcasted_iota(jnp.int32, (8, LANES), 0)
    lane = lax.broadcasted_iota(jnp.int32, (8, LANES), 1)
    own_row = sub == lane >> 4
    first_lane = lax.broadcasted_iota(jnp.int32, (SLAB, POINTS), 1) == 0

    row_of = lax.broadcasted_iota(jnp.int32, (32, 2 * LANES), 0)
    lane_of = lax.broadcasted_iota(jnp.int32, (LANES, 2 * LANES), 0).astype(BF16)

    def gather_pair(pair, carry):
        first, second = 2 * pair, 2 * pair + 1
        routes = [lists[r, 0].astype(jnp.int32) for r in (first, second)]
        last = jnp.maximum(extent[first] & 3, extent[second] & 3)
        for s in range(4):

            @pl.when(last >= s)
            def _():
                for g in range(groups):
                    k = 8 * s + g
                    route = jnp.concatenate([a[k : k + 1, :] for a in routes], axis=1)
                    lane_spot = (route & (LANES - 1)).astype(F32).astype(BF16)
                    onehot = jnp.where(lane_of == lane_spot, BF16(1), BF16(0))
                    rows = jnp.dot(
                        volts[g].reshape(64, LANES),
                        onehot,
                        preferred_element_type=F32,
                    )
                    hit = row_of == (route >> 7)
                    for i in range(2):
                        entry = jnp.sum(
                            jnp.where(hit, rows[32 * i : 32 * i + 32], 0.0),
                            axis=0,
                            keepdims=True,
                        )
                        slots[i, first, k : k + 1, :] = entry[:, :LANES]
                        slots[i, second, k : k + 1, :] = entry[:, LANES:]

        return carry

    lax.fori_loop(0, slabs // 2, gather_pair, 0)

    def convolve(r):
        here = lax.rem(r + 3, 3)
        before = lax.rem(r + 2, 3)
        for i in range(2):
            sums = []
            for q in range(RADIX):
                rows = [cells[here, 2 * q + i], cells[before, 2 * q + i]]
                sums.append(
                    jnp.dot(
                        bands[...],
                        jnp.concatenate(rows + rows, axis=0),
                        preferred_element_type=F32,
                    )
                )
            for qx in range(RADIX):
                terms = [
                    sums[(qx - kx) % RADIX][kx * SLAB : (kx + 1) * SLAB]
                    for kx in range(KERNEL_SIDE)
                ]
                total = sum(terms[1 : qx + 1], terms[0])
                if qx < KERNEL_SIDE - 1:
                    spill = sum(terms[qx + 2 :], terms[qx + 1])
                    spill = pltpu.roll(spill, 1, 1)
                    total = total + jnp.where(first_lane, 0.0, spill)
                total = total.astype(BF16)
                at = (2 * qx + i) * POINTS
                for qy in range(RADIX):
                    row = pl.multiple_of(qy * POINTS + slab_points * jnp.maximum(r, 0), 16)
                    aperture[pl.ds(row, 16), at : at + POINTS] = total[
                        16 * qy : 16 * qy + 16
                    ]

    def grid_chunks(r, chunks, list_rows):
        convolve(r - 1)
        place = lax.rem(r, 3)
        size = 8 * chunks
        members = lists[r, 1].astype(jnp.int32)[:size]
        columns = lists[r, 2].astype(jnp.int32)[:size]
        member_lane = members & (LANES - 1)
        member_row = members >> 7
        values = [jnp.zeros((size, LANES), F32)] * 2
        for k in range(list_rows):
            hit = member_row == k
            for i in range(2):
                row = jnp.broadcast_to(slots[i, r, k : k + 1, :], (size, LANES))
                values[i] = jnp.where(hit, pick(row, member_lane), values[i])
        kind = (columns & (RADIX - 1)) + RADIX * (columns >> 9)
        point = ((columns >> 2) & (LANES - 1)).astype(F32)
        cell = lax.broadcasted_iota(jnp.int32, (LANES, chunks * LANES), 0).astype(BF16)
        for qy in range(RADIX):
            placed = []
            for h in range(2):
                at = [8 * c + 2 * qy + h for c in range(chunks)]
                kinds = [
                    jnp.where(
                        own_row, jnp.broadcast_to(kind[a : a + 1, :], (8, LANES)), -1
                    )
                    for a in at
                ]
                spread = [
                    [jnp.broadcast_to(v[a : a + 1, :], (8, LANES)) for a in at]
                    for v in values
                ]
                left = jnp.concatenate(
                    [
                        jnp.concatenate(
                            [
                                jnp.where(kinds[c] == plane, spread[i][c], 0.0)
                                for c in range(chunks)
                            ],
                            axis=1,
                        )
                        for plane in range(2 * RADIX)
                        for i in range(2)
                    ],
                    axis=0,
                ).astype(BF16)
                spot = jnp.concatenate([point[a : a + 1, :] for a in at], axis=1)
                onehot = jnp.where(cell == spot.astype(BF16), BF16(1), BF16(0))
                placed.append(
                    lax.dot_general(
                        left,
                        onehot,
                        (((1,), (1,)), ((), ())),
                        preferred_element_type=F32,
                    )
                )
            for half in range(2):
                for plane in range(2 * RADIX):
                    a = (half * 2 * RADIX + plane) * 8
                    cells[
                        place,
                        plane,
                        16 * qy : 16 * qy + 16,
                        half * LANES : (half + 1) * LANES,
                    ] = jnp.concatenate([p[a : a + 8, :] for p in placed], axis=0).astype(
                        BF16
                    )

    def grid_slab(r, carry):
        @pl.when(extent[r] < 4)
        def _():
            grid_chunks(r, 2, 16)

        @pl.when(extent[r] >= 4)
        def _():
            grid_chunks(r, 4, 32)

        return carry

    lax.fori_loop(0, slabs, grid_slab, 0)
    convolve(slabs - 1)

    def row_transform(qy, carry):
        rows = pl.ds(pl.multiple_of(qy * POINTS, POINTS), POINTS)
        parts = [
            lax.dot_general(
                wide[q],
                aperture[rows, 2 * q * POINTS : 2 * (q + 1) * POINTS],
                (((1,), (1,)), ((), ())),
                preferred_element_type=F32,
            )
            for q in range(RADIX)
        ]
        re, im = butterfly(
            [part[:POINTS] for part in parts], [part[POINTS:] for part in parts]
        )
        at = pl.multiple_of(qy * 2 * POINTS, 2 * POINTS)
        for m in range(RADIX):
            spectrum[m * POINTS : (m + 1) * POINTS, pl.ds(at, POINTS)] = re[m].astype(
                BF16
            )
            spectrum[
                m * POINTS : (m + 1) * POINTS, pl.ds(at + POINTS, POINTS)
            ] = im[m].astype(BF16)
        return carry

    wide_copy.wait()
    lax.fori_loop(0, RADIX, row_transform, 0, unroll=True)

    def hand_over(n):
        rows = pl.ds(n * POINTS, POINTS)
        return pltpu.make_async_copy(power.at[rows], power_to.at[rows], left_for.at[n])

    def column_transform(n, carry):
        rows = pl.ds(n * POINTS, POINTS)
        parts = [
            jnp.dot(
                spectrum[rows, 2 * q * POINTS : 2 * (q + 1) * POINTS],
                tall[q],
                preferred_element_type=F32,
            )
            for q in range(RADIX)
        ]
        re, im = butterfly(
            [part[:, :POINTS] for part in parts], [part[:, POINTS:] for part in parts]
        )
        for m in range(RADIX):
            power[rows, m * POINTS : (m + 1) * POINTS] = (
                re[m] * re[m] + im[m] * im[m]
            ).astype(BF16)
        return carry

    tall_copy.wait()
    for n in range(RADIX):
        column_transform(n, 0)
        hand_over(n).start()
    for n in range(RADIX):
        hand_over(n).wait()


def sample_power(taps, extent, volts, lists, wide, tall):
    return pl.pallas_call(
        sample_kernel,
        out_shape=jax.ShapeDtypeStruct((NGRID, NGRID), BF16),
        in_specs=[pl.BlockSpec(memory_space=pltpu.SMEM)] * 2
        + [pl.BlockSpec(memory_space=pltpu.VMEM)] * 2
        + [pl.BlockSpec(memory_space=pl.ANY)] * 2,
        out_specs=pl.BlockSpec(memory_space=pl.ANY),
        scratch_shapes=[
            pltpu.VMEM((2, lists.shape[0], 32, LANES), F32),
            pltpu.VMEM((4 * SLAB, 4 * SLAB), BF16),
            pltpu.VMEM((3, 2 * RADIX, SLAB, POINTS), BF16),
            pltpu.VMEM((NGRID, 2 * NGRID), BF16),
            pltpu.VMEM((NGRID, 2 * NGRID), BF16),
            pltpu.VMEM(wide.shape, BF16),
            pltpu.VMEM(tall.shape, BF16),
            pltpu.VMEM((NGRID, NGRID), BF16),
            pltpu.SemaphoreType.DMA((2,)),
            pltpu.SemaphoreType.DMA((RADIX,)),
        ],
        compiler_params=pltpu.CompilerParams(vmem_limit_bytes=56 * 2**20),
    )(taps, extent, volts, lists, wide, tall)


def slab_lists(route_lists, row_members, row_counts, anchor_cols):
    routes = route_lists[:, 0, :].reshape(8, 4, LANES).transpose(1, 0, 2)
    slot = ((row_members >> 7) & 3) * 1024 + (row_members >> 9) * LANES
    slot = slot + (row_members & (LANES - 1))
    live = jnp.arange(row_members.shape[1], dtype=jnp.int32)[None, :] < row_counts[:, None]
    slot = jnp.where(live, slot, -1)
    ordered = [
        a.reshape(2, 8, RADIX, 4, 16).transpose(3, 2, 0, 1, 4).reshape(32, LANES)
        for a in (slot, anchor_cols)
    ]
    return jnp.stack([routes.reshape(32, LANES), *ordered]).astype(jnp.int16)


def list_extents(lists):
    slot = lists[:, 1].astype(jnp.int32)
    top = jnp.max(slot, axis=(1, 2))
    late = jnp.max(slot[:, 16:], axis=(1, 2))
    wide = (top >= 2048) | (late >= 0)
    return (jnp.maximum(top, 0) >> 10) + jnp.where(wide, 4, 0)


def per_device(voltages, kernel, route_lists, row_members, row_counts, anchor_cols):
    chan_count = lax.axis_size("chan")
    row_count = lax.axis_size("row")
    group_size = voltages.shape[3]
    samples = voltages.shape[1]
    lists = slab_lists(route_lists, row_members, row_counts, anchor_cols)
    lists = jnp.broadcast_to(lists[None], (row_count,) + lists.shape)
    lists = lax.all_to_all(lists, "row", split_axis=0, concat_axis=0, tiled=True)
    mine = lax.dynamic_index_in_dim(voltages, lax.axis_index("row"), 1, keepdims=False)
    mine = mine.reshape(chan_count, 2, group_size // LANES, LANES)
    volts = lax.all_to_all(mine, "chan", split_axis=0, concat_axis=0, tiled=True)
    wide, tall = stage_tables()
    power = sample_power(
        kernel[0],
        list_extents(lists),
        volts,
        lists,
        jnp.asarray(wide),
        jnp.asarray(tall),
    )
    power = power.reshape(row_count, NGRID // row_count, NGRID)
    power = lax.all_to_all(power, "row", split_axis=0, concat_axis=0, tiled=True)
    scale_factor = 1.0 / (group_size * chan_count * samples * KERNEL_SIDE * KERNEL_SIDE)
    sky_image = jnp.sum(power.astype(F32), axis=0) * scale_factor
    return sky_image.T[None]


def solution(mesh):
    in_specs = (
        P(None, None, None, "chan"),
        P("chan", None, None),
        P(None, "row", None),
        P("row", None),
        P("row"),
        P("row", None),
    )
    out_specs = P("chan", None, "row")
    return jax.shard_map(
        per_device, mesh=mesh, in_specs=in_specs, out_specs=out_specs, check_vma=False
    )
```

```python
import jax
import jax.numpy as jnp
import numpy as np
from jax import lax
from jax.experimental import pallas as pl
from jax.experimental.pallas import tpu as pltpu
from jax.sharding import PartitionSpec as P

NGRID = 1024
KERNEL_SIDE = 4
SLAB = 64
RADIX = 4
POINTS = NGRID // RADIX
LANES = 128
F32 = jnp.float32
BF16 = jnp.bfloat16


def stage_tables():
    n = np.arange(NGRID, dtype=np.int64)
    product = (n[:, None] * n[None, :POINTS]) % NGRID
    angles = product.astype(np.float32) * np.float32(-2.0 * np.pi / NGRID)
    cos = np.cos(angles).astype(np.float32)
    sin = np.sin(angles).astype(np.float32)
    parts = []
    for q in range(RADIX):
        c, s = cos[q::RADIX], sin[q::RADIX]
        parts.append(np.block([[c, s], [-s, c]]))
    table = np.stack(parts)
    return (
        np.ascontiguousarray(table.transpose(0, 2, 1)).astype(jnp.bfloat16),
        table.astype(jnp.bfloat16),
    )


def butterfly(re, im):
    ra, rb = re[0] + re[2], re[0] - re[2]
    rc, rd = re[1] + re[3], re[1] - re[3]
    ia, ib = im[0] + im[2], im[0] - im[2]
    ic, id_ = im[1] + im[3], im[1] - im[3]
    return (ra + rc, rb + id_, ra - rc, rb - id_), (ia + ic, ib - rd, ia - ic, ib + rd)


def pick(table_rows, index):
    return jnp.take_along_axis(table_rows, index, axis=1, mode="promise_in_bounds")


def sample_kernel(
    taps, extent, volts, lists, wide_from, tall_from, power_to, slots, bands, cells, aperture,
    spectrum, wide, tall, power, arrived, left_for,
):
    slabs = lists.shape[0]
    groups = volts.shape[0]
    slab_points = POINTS // slabs
    wide_copy = pltpu.make_async_copy(wide_from, wide, arrived.at[0])
    tall_copy = pltpu.make_async_copy(tall_from, tall, arrived.at[1])
    wide_copy.start()
    tall_copy.start()

    down = lax.broadcasted_iota(jnp.int32, (SLAB, 4 * SLAB), 0)
    across = lax.broadcasted_iota(jnp.int32, (SLAB, 4 * SLAB), 1)
    apart = RADIX * (down & 15) + (down >> 4)
    apart = apart - RADIX * (across & 15) - ((across >> 4) & 3)
    apart = apart + SLAB * ((across >> 6) & 1)
    for kx in range(KERNEL_SIDE):
        tap = jnp.zeros((SLAB, 4 * SLAB), F32)
        for ky in range(KERNEL_SIDE):
            tap = jnp.where(apart == ky, taps[ky, kx], tap)
        high = tap.astype(BF16).astype(F32)
        bands[kx * SLAB : (kx + 1) * SLAB, :] = jnp.where(
            across < 2 * SLAB, high, tap - high
        ).astype(BF16)
    cells[2] = jnp.zeros(cells.shape[1:], BF16)

    sub = lax.broadcasted_iota(jnp.int32, (8, LANES), 0)
    lane = lax.broadcasted_iota(jnp.int32, (8, LANES), 1)
    own_row = sub == lane >> 4
    first_lane = lax.broadcasted_iota(jnp.int32, (SLAB, POINTS), 1) == 0

    row_of = lax.broadcasted_iota(jnp.int32, (32, 2 * LANES), 0)
    lane_of = lax.broadcasted_iota(jnp.int32, (LANES, 2 * LANES), 0).astype(BF16)

    def gather_pair(pair, carry):
        first, second = 2 * pair, 2 * pair + 1
        routes = [lists[r, 0].astype(jnp.int32) for r in (first, second)]
        last = jnp.maximum(extent[first] & 3, extent[second] & 3)
        for s in range(4):

            @pl.when(last >= s)
            def _():
                for g in range(groups):
                    k = 8 * s + g
                    route = jnp.concatenate([a[k : k + 1, :] for a in routes], axis=1)
                    lane_spot = (route & (LANES - 1)).astype(F32).astype(BF16)
                    onehot = jnp.where(lane_of == lane_spot, BF16(1), BF16(0))
                    rows = jnp.dot(
                        volts[g].reshape(64, LANES),
                        onehot,
                        preferred_element_type=F32,
                    )
                    hit = row_of == (route >> 7)
                    for i in range(2):
                        entry = jnp.sum(
                            jnp.where(hit, rows[32 * i : 32 * i + 32], 0.0),
                            axis=0,
                            keepdims=True,
                        )
                        slots[i, first, k : k + 1, :] = entry[:, :LANES]
                        slots[i, second, k : k + 1, :] = entry[:, LANES:]

        return carry

    lax.fori_loop(0, slabs // 2, gather_pair, 0)

    def convolve(r):
        here = lax.rem(r + 3, 3)
        before = lax.rem(r + 2, 3)
        for i in range(2):
            sums = []
            for q in range(RADIX):
                rows = [cells[here, 2 * q + i], cells[before, 2 * q + i]]
                sums.append(
                    jnp.dot(
                        bands[...],
                        jnp.concatenate(rows + rows, axis=0),
                        preferred_element_type=F32,
                    )
                )
            for qx in range(RADIX):
                terms = [
                    sums[(qx - kx) % RADIX][kx * SLAB : (kx + 1) * SLAB]
                    for kx in range(KERNEL_SIDE)
                ]
                total = sum(terms[1 : qx + 1], terms[0])
                if qx < KERNEL_SIDE - 1:
                    spill = sum(terms[qx + 2 :], terms[qx + 1])
                    spill = pltpu.roll(spill, 1, 1)
                    total = total + jnp.where(first_lane, 0.0, spill)
                total = total.astype(BF16)
                at = (2 * qx + i) * POINTS
                for qy in range(RADIX):
                    row = pl.multiple_of(qy * POINTS + slab_points * jnp.maximum(r, 0), 16)
                    aperture[pl.ds(row, 16), at : at + POINTS] = total[
                        16 * qy : 16 * qy + 16
                    ]

    def grid_chunks(r, chunks, list_rows):
        convolve(r - 1)
        place = lax.rem(r, 3)
        size = 8 * chunks
        members = lists[r, 1].astype(jnp.int32)[:size]
        columns = lists[r, 2].astype(jnp.int32)[:size]
        member_lane = members & (LANES - 1)
        member_row = members >> 7
        values = [jnp.zeros((size, LANES), F32)] * 2
        for k in range(list_rows):
            hit = member_row == k
            for i in range(2):
                row = jnp.broadcast_to(slots[i, r, k : k + 1, :], (size, LANES))
                values[i] = jnp.where(hit, pick(row, member_lane), values[i])
        kind = (columns & (RADIX - 1)) + RADIX * (columns >> 9)
        point = ((columns >> 2) & (LANES - 1)).astype(F32)
        cell = lax.broadcasted_iota(jnp.int32, (LANES, chunks * LANES), 0).astype(BF16)
        for qy in range(RADIX):
            placed = []
            for h in range(2):
                at = [8 * c + 2 * qy + h for c in range(chunks)]
                kinds = [
                    jnp.where(
                        own_row, jnp.broadcast_to(kind[a : a + 1, :], (8, LANES)), -1
                    )
                    for a in at
                ]
                spread = [
                    [jnp.broadcast_to(v[a : a + 1, :], (8, LANES)) for a in at]
                    for v in values
                ]
                left = jnp.concatenate(
                    [
                        jnp.concatenate(
                            [
                                jnp.where(kinds[c] == plane, spread[i][c], 0.0)
                                for c in range(chunks)
                            ],
                            axis=1,
                        )
                        for plane in range(2 * RADIX)
                        for i in range(2)
                    ],
                    axis=0,
                ).astype(BF16)
                spot = jnp.concatenate([point[a : a + 1, :] for a in at], axis=1)
                onehot = jnp.where(cell == spot.astype(BF16), BF16(1), BF16(0))
                placed.append(
                    lax.dot_general(
                        left,
                        onehot,
                        (((1,), (1,)), ((), ())),
                        preferred_element_type=F32,
                    )
                )
            for half in range(2):
                for plane in range(2 * RADIX):
                    a = (half * 2 * RADIX + plane) * 8
                    cells[
                        place,
                        plane,
                        16 * qy : 16 * qy + 16,
                        half * LANES : (half + 1) * LANES,
                    ] = jnp.concatenate([p[a : a + 8, :] for p in placed], axis=0).astype(
                        BF16
                    )

    def grid_slab(r, carry):
        @pl.when(extent[r] < 4)
        def _():
            grid_chunks(r, 2, 16)

        @pl.when(extent[r] >= 4)
        def _():
            grid_chunks(r, 4, 32)

        return carry

    lax.fori_loop(0, slabs, grid_slab, 0)
    convolve(slabs - 1)

    def row_transform(qy, carry):
        rows = pl.ds(pl.multiple_of(qy * POINTS, POINTS), POINTS)
        parts = [
            lax.dot_general(
                wide[q],
                aperture[rows, 2 * q * POINTS : 2 * (q + 1) * POINTS],
                (((1,), (1,)), ((), ())),
                preferred_element_type=F32,
            )
            for q in range(RADIX)
        ]
        re, im = butterfly(
            [part[:POINTS] for part in parts], [part[POINTS:] for part in parts]
        )
        at = pl.multiple_of(qy * 2 * POINTS, 2 * POINTS)
        for m in range(RADIX):
            spectrum[m * POINTS : (m + 1) * POINTS, pl.ds(at, POINTS)] = re[m].astype(
                BF16
            )
            spectrum[
                m * POINTS : (m + 1) * POINTS, pl.ds(at + POINTS, POINTS)
            ] = im[m].astype(BF16)
        return carry

    wide_copy.wait()
    lax.fori_loop(0, RADIX, row_transform, 0, unroll=True)

    def hand_over(n):
        rows = pl.ds(n * POINTS, POINTS)
        return pltpu.make_async_copy(power.at[rows], power_to.at[rows], left_for.at[n])

    def column_transform(n, carry):
        rows = pl.ds(n * POINTS, POINTS)
        parts = [
            jnp.dot(
                spectrum[rows, 2 * q * POINTS : 2 * (q + 1) * POINTS],
                tall[q],
                preferred_element_type=F32,
            )
            for q in range(RADIX)
        ]
        re, im = butterfly(
            [part[:, :POINTS] for part in parts], [part[:, POINTS:] for part in parts]
        )
        for m in range(RADIX):
            power[rows, m * POINTS : (m + 1) * POINTS] = (
                re[m] * re[m] + im[m] * im[m]
            ).astype(BF16)
        return carry

    tall_copy.wait()
    for n in range(RADIX):
        column_transform(n, 0)
        hand_over(n).start()
    for n in range(RADIX):
        hand_over(n).wait()


def sample_power(taps, extent, volts, lists, wide, tall):
    return pl.pallas_call(
        sample_kernel,
        out_shape=jax.ShapeDtypeStruct((NGRID, NGRID), BF16),
        in_specs=[pl.BlockSpec(memory_space=pltpu.SMEM)] * 2
        + [pl.BlockSpec(memory_space=pltpu.VMEM)] * 2
        + [pl.BlockSpec(memory_space=pl.ANY)] * 2,
        out_specs=pl.BlockSpec(memory_space=pl.ANY),
        scratch_shapes=[
            pltpu.VMEM((2, lists.shape[0], 32, LANES), F32),
            pltpu.VMEM((4 * SLAB, 4 * SLAB), BF16),
            pltpu.VMEM((3, 2 * RADIX, SLAB, POINTS), BF16),
            pltpu.VMEM((NGRID, 2 * NGRID), BF16),
            pltpu.VMEM((NGRID, 2 * NGRID), BF16),
            pltpu.VMEM(wide.shape, BF16),
            pltpu.VMEM(tall.shape, BF16),
            pltpu.VMEM((NGRID, NGRID), BF16),
            pltpu.SemaphoreType.DMA((2,)),
            pltpu.SemaphoreType.DMA((RADIX,)),
        ],
        compiler_params=pltpu.CompilerParams(vmem_limit_bytes=56 * 2**20),
    )(taps, extent, volts, lists, wide, tall)


def slab_lists(route_lists, row_members, row_counts, anchor_cols):
    routes = route_lists[:, 0, :].reshape(8, 4, LANES).transpose(1, 0, 2)
    slot = ((row_members >> 7) & 3) * 1024 + (row_members >> 9) * LANES
    slot = slot + (row_members & (LANES - 1))
    live = jnp.arange(row_members.shape[1], dtype=jnp.int32)[None, :] < row_counts[:, None]
    slot = jnp.where(live, slot, -1)
    ordered = [
        a.reshape(2, 8, RADIX, 4, 16).transpose(3, 2, 0, 1, 4).reshape(32, LANES)
        for a in (slot, anchor_cols)
    ]
    return jnp.stack([routes.reshape(32, LANES), *ordered]).astype(jnp.int16)


def list_extents(lists):
    slot = lists[:, 1].astype(jnp.int32)
    top = jnp.max(slot, axis=(1, 2))
    late = jnp.max(slot[:, 16:], axis=(1, 2))
    wide = (top >= 2048) | (late >= 0)
    return (jnp.maximum(top, 0) >> 10) + jnp.where(wide, 4, 0)


def per_device(voltages, kernel, route_lists, row_members, row_counts, anchor_cols):
    chan_count = lax.axis_size("chan")
    row_count = lax.axis_size("row")
    group_size = voltages.shape[3]
    samples = voltages.shape[1]
    mine = lax.dynamic_index_in_dim(voltages, lax.axis_index("row"), 1, keepdims=False)
    mine = mine.reshape(chan_count, 2, group_size // LANES, LANES)
    volts = lax.all_to_all(mine, "chan", split_axis=0, concat_axis=0, tiled=True)
    lists = slab_lists(route_lists, row_members, row_counts, anchor_cols)
    lists = jnp.broadcast_to(lists[None], (row_count,) + lists.shape)
    volts, lists = lax.optimization_barrier((volts, lists))
    lists = lax.all_to_all(lists, "row", split_axis=0, concat_axis=0, tiled=True)
    wide, tall = stage_tables()
    power = sample_power(
        kernel[0],
        list_extents(lists),
        volts,
        lists,
        jnp.asarray(wide),
        jnp.asarray(tall),
    )
    power = power.reshape(row_count, NGRID // row_count, NGRID)
    power = lax.all_to_all(power, "row", split_axis=0, concat_axis=0, tiled=True)
    scale_factor = 1.0 / (group_size * chan_count * samples * KERNEL_SIDE * KERNEL_SIDE)
    sky_image = jnp.sum(power.astype(F32), axis=0) * scale_factor
    return sky_image.T[None]


def solution(mesh):
    in_specs = (
        P(None, None, None, "chan"),
        P("chan", None, None),
        P(None, "row", None),
        P("row", None),
        P("row"),
        P("row", None),
    )
    out_specs = P("chan", None, "row")
    return jax.shard_map(
        per_device, mesh=mesh, in_specs=in_specs, out_specs=out_specs, check_vma=False
    )
```

```python
import jax
import jax.numpy as jnp
import numpy as np
from jax import lax
from jax.experimental import pallas as pl
from jax.experimental.pallas import tpu as pltpu
from jax.sharding import PartitionSpec as P

NGRID = 1024
KERNEL_SIDE = 4
SLAB = 64
RADIX = 4
POINTS = NGRID // RADIX
LANES = 128
F32 = jnp.float32
BF16 = jnp.bfloat16


def stage_tables():
    n = np.arange(NGRID, dtype=np.int64)
    product = (n[:, None] * n[None, :POINTS]) % NGRID
    angles = product.astype(np.float32) * np.float32(-2.0 * np.pi / NGRID)
    cos = np.cos(angles).astype(np.float32)
    sin = np.sin(angles).astype(np.float32)
    parts = []
    for q in range(RADIX):
        c, s = cos[q::RADIX], sin[q::RADIX]
        parts.append(np.block([[c, s], [-s, c]]))
    table = np.stack(parts)
    return (
        np.ascontiguousarray(table.transpose(0, 2, 1)).astype(jnp.bfloat16),
        table.astype(jnp.bfloat16),
    )


def butterfly(re, im):
    ra, rb = re[0] + re[2], re[0] - re[2]
    rc, rd = re[1] + re[3], re[1] - re[3]
    ia, ib = im[0] + im[2], im[0] - im[2]
    ic, id_ = im[1] + im[3], im[1] - im[3]
    return (ra + rc, rb + id_, ra - rc, rb - id_), (ia + ic, ib - rd, ia - ic, ib + rd)


def pick(table_rows, index):
    return jnp.take_along_axis(table_rows, index, axis=1, mode="promise_in_bounds")


def sample_kernel(
    taps, extent, volts, lists, wide_from, tall_from, power_to, slots, bands, cells, aperture,
    spectrum, wide, tall, power, arrived, left_for,
):
    slabs = lists.shape[0]
    groups = volts.shape[0]
    slab_points = POINTS // slabs
    wide_copy = pltpu.make_async_copy(wide_from, wide, arrived.at[0])
    tall_copy = pltpu.make_async_copy(tall_from, tall, arrived.at[1])
    wide_copy.start()
    tall_copy.start()

    down = lax.broadcasted_iota(jnp.int32, (SLAB, 4 * SLAB), 0)
    across = lax.broadcasted_iota(jnp.int32, (SLAB, 4 * SLAB), 1)
    apart = RADIX * (down & 15) + (down >> 4)
    apart = apart - RADIX * (across & 15) - ((across >> 4) & 3)
    apart = apart + SLAB * ((across >> 6) & 1)
    for kx in range(KERNEL_SIDE):
        tap = jnp.zeros((SLAB, 4 * SLAB), F32)
        for ky in range(KERNEL_SIDE):
            tap = jnp.where(apart == ky, taps[ky, kx], tap)
        high = tap.astype(BF16).astype(F32)
        bands[kx * SLAB : (kx + 1) * SLAB, :] = jnp.where(
            across < 2 * SLAB, high, tap - high
        ).astype(BF16)
    cells[2] = jnp.zeros(cells.shape[1:], BF16)

    sub = lax.broadcasted_iota(jnp.int32, (8, LANES), 0)
    lane = lax.broadcasted_iota(jnp.int32, (8, LANES), 1)
    own_row = sub == lane >> 4
    first_lane = lax.broadcasted_iota(jnp.int32, (SLAB, POINTS), 1) == 0

    row_of = lax.broadcasted_iota(jnp.int32, (32, 2 * LANES), 0)
    lane_of = lax.broadcasted_iota(jnp.int32, (LANES, 2 * LANES), 0).astype(BF16)

    def gather_pair(pair, carry):
        first, second = 2 * pair, 2 * pair + 1
        routes = [lists[r, 0].astype(jnp.int32) for r in (first, second)]
        last = jnp.maximum(extent[first], extent[second])
        for s in range(4):

            @pl.when(last >= s)
            def _():
                for g in range(groups):
                    k = 8 * s + g
                    route = jnp.concatenate([a[k : k + 1, :] for a in routes], axis=1)
                    lane_spot = (route & (LANES - 1)).astype(F32).astype(BF16)
                    onehot = jnp.where(lane_of == lane_spot, BF16(1), BF16(0))
                    rows = jnp.dot(
                        volts[g].reshape(64, LANES),
                        onehot,
                        preferred_element_type=F32,
                    )
                    hit = row_of == (route >> 7)
                    for i in range(2):
                        entry = jnp.sum(
                            jnp.where(hit, rows[32 * i : 32 * i + 32], 0.0),
                            axis=0,
                            keepdims=True,
                        )
                        slots[i, first, k : k + 1, :] = entry[:, :LANES]
                        slots[i, second, k : k + 1, :] = entry[:, LANES:]

        return carry

    lax.fori_loop(0, slabs // 2, gather_pair, 0)

    def convolve(r):
        here = lax.rem(r + 3, 3)
        before = lax.rem(r + 2, 3)
        for i in range(2):
            sums = []
            for q in range(RADIX):
                rows = [cells[here, 2 * q + i], cells[before, 2 * q + i]]
                sums.append(
                    jnp.dot(
                        bands[...],
                        jnp.concatenate(rows + rows, axis=0),
                        preferred_element_type=F32,
                    )
                )
            for qx in range(RADIX):
                terms = [
                    sums[(qx - kx) % RADIX][kx * SLAB : (kx + 1) * SLAB]
                    for kx in range(KERNEL_SIDE)
                ]
                total = sum(terms[1 : qx + 1], terms[0])
                if qx < KERNEL_SIDE - 1:
                    spill = sum(terms[qx + 2 :], terms[qx + 1])
                    spill = pltpu.roll(spill, 1, 1)
                    total = total + jnp.where(first_lane, 0.0, spill)
                total = total.astype(BF16)
                at = (2 * qx + i) * POINTS
                for qy in range(RADIX):
                    row = pl.multiple_of(qy * POINTS + slab_points * jnp.maximum(r, 0), 16)
                    aperture[pl.ds(row, 16), at : at + POINTS] = total[
                        16 * qy : 16 * qy + 16
                    ]

    def grid_chunks(r, chunks, list_rows):
        convolve(r - 1)
        place = lax.rem(r, 3)
        size = 8 * chunks
        members = lists[r, 1].astype(jnp.int32)[:size]
        columns = lists[r, 2].astype(jnp.int32)[:size]
        member_lane = members & (LANES - 1)
        member_row = members >> 7
        values = [jnp.zeros((size, LANES), F32)] * 2
        for k in range(list_rows):
            hit = member_row == k
            for i in range(2):
                row = jnp.broadcast_to(slots[i, r, k : k + 1, :], (size, LANES))
                values[i] = jnp.where(hit, pick(row, member_lane), values[i])
        kind = (columns & (RADIX - 1)) + RADIX * (columns >> 9)
        point = ((columns >> 2) & (LANES - 1)).astype(F32)
        cell = lax.broadcasted_iota(jnp.int32, (LANES, chunks * LANES), 0).astype(BF16)
        for qy in range(RADIX):
            placed = []
            for h in range(2):
                at = [8 * c + 2 * qy + h for c in range(chunks)]
                kinds = [
                    jnp.where(
                        own_row, jnp.broadcast_to(kind[a : a + 1, :], (8, LANES)), -1
                    )
                    for a in at
                ]
                spread = [
                    [jnp.broadcast_to(v[a : a + 1, :], (8, LANES)) for a in at]
                    for v in values
                ]
                left = jnp.concatenate(
                    [
                        jnp.concatenate(
                            [
                                jnp.where(kinds[c] == plane, spread[i][c], 0.0)
                                for c in range(chunks)
                            ],
                            axis=1,
                        )
                        for plane in range(2 * RADIX)
                        for i in range(2)
                    ],
                    axis=0,
                ).astype(BF16)
                spot = jnp.concatenate([point[a : a + 1, :] for a in at], axis=1)
                onehot = jnp.where(cell == spot.astype(BF16), BF16(1), BF16(0))
                placed.append(
                    lax.dot_general(
                        left,
                        onehot,
                        (((1,), (1,)), ((), ())),
                        preferred_element_type=F32,
                    )
                )
            for half in range(2):
                for plane in range(2 * RADIX):
                    a = (half * 2 * RADIX + plane) * 8
                    cells[
                        place,
                        plane,
                        16 * qy : 16 * qy + 16,
                        half * LANES : (half + 1) * LANES,
                    ] = jnp.concatenate([p[a : a + 8, :] for p in placed], axis=0).astype(
                        BF16
                    )

    def grid_slab(r, carry):
        @pl.when(extent[r] < 2)
        def _():
            grid_chunks(r, 2, 16)

        @pl.when(extent[r] >= 2)
        def _():
            grid_chunks(r, 4, 32)

        return carry

    lax.fori_loop(0, slabs, grid_slab, 0)
    convolve(slabs - 1)

    def row_transform(qy, carry):
        rows = pl.ds(pl.multiple_of(qy * POINTS, POINTS), POINTS)
        parts = [
            lax.dot_general(
                wide[q],
                aperture[rows, 2 * q * POINTS : 2 * (q + 1) * POINTS],
                (((1,), (1,)), ((), ())),
                preferred_element_type=F32,
            )
            for q in range(RADIX)
        ]
        re, im = butterfly(
            [part[:POINTS] for part in parts], [part[POINTS:] for part in parts]
        )
        at = pl.multiple_of(qy * 2 * POINTS, 2 * POINTS)
        for m in range(RADIX):
            spectrum[m * POINTS : (m + 1) * POINTS, pl.ds(at, POINTS)] = re[m].astype(
                BF16
            )
            spectrum[
                m * POINTS : (m + 1) * POINTS, pl.ds(at + POINTS, POINTS)
            ] = im[m].astype(BF16)
        return carry

    wide_copy.wait()
    lax.fori_loop(0, RADIX, row_transform, 0, unroll=True)

    def hand_over(n):
        rows = pl.ds(n * POINTS, POINTS)
        return pltpu.make_async_copy(power.at[rows], power_to.at[rows], left_for.at[n])

    def column_transform(n, carry):
        rows = pl.ds(n * POINTS, POINTS)
        parts = [
            jnp.dot(
                spectrum[rows, 2 * q * POINTS : 2 * (q + 1) * POINTS],
                tall[q],
                preferred_element_type=F32,
            )
            for q in range(RADIX)
        ]
        re, im = butterfly(
            [part[:, :POINTS] for part in parts], [part[:, POINTS:] for part in parts]
        )
        for m in range(RADIX):
            power[rows, m * POINTS : (m + 1) * POINTS] = (
                re[m] * re[m] + im[m] * im[m]
            ).astype(BF16)
        return carry

    tall_copy.wait()
    for n in range(RADIX):
        column_transform(n, 0)
        hand_over(n).start()
    for n in range(RADIX):
        hand_over(n).wait()


def sample_power(taps, extent, volts, lists, wide, tall):
    return pl.pallas_call(
        sample_kernel,
        out_shape=jax.ShapeDtypeStruct((NGRID, NGRID), BF16),
        in_specs=[pl.BlockSpec(memory_space=pltpu.SMEM)] * 2
        + [pl.BlockSpec(memory_space=pltpu.VMEM)] * 2
        + [pl.BlockSpec(memory_space=pl.ANY)] * 2,
        out_specs=pl.BlockSpec(memory_space=pl.ANY),
        scratch_shapes=[
            pltpu.VMEM((2, lists.shape[0], 32, LANES), F32),
            pltpu.VMEM((4 * SLAB, 4 * SLAB), BF16),
            pltpu.VMEM((3, 2 * RADIX, SLAB, POINTS), BF16),
            pltpu.VMEM((NGRID, 2 * NGRID), BF16),
            pltpu.VMEM((NGRID, 2 * NGRID), BF16),
            pltpu.VMEM(wide.shape, BF16),
            pltpu.VMEM(tall.shape, BF16),
            pltpu.VMEM((NGRID, NGRID), BF16),
            pltpu.SemaphoreType.DMA((2,)),
            pltpu.SemaphoreType.DMA((RADIX,)),
        ],
        compiler_params=pltpu.CompilerParams(vmem_limit_bytes=56 * 2**20),
    )(taps, extent, volts, lists, wide, tall)


def slab_lists(route_lists, row_members, row_counts, anchor_cols):
    routes = route_lists[:, 0, :].reshape(8, 4, LANES).transpose(1, 0, 2)
    slot = ((row_members >> 7) & 3) * 1024 + (row_members >> 9) * LANES
    slot = slot + (row_members & (LANES - 1))
    live = jnp.arange(row_members.shape[1], dtype=jnp.int32)[None, :] < row_counts[:, None]
    slot = jnp.where(live, slot, -1)
    ordered = [
        a.reshape(2, 8, RADIX, 4, 16).transpose(3, 2, 0, 1, 4).reshape(32, LANES)
        for a in (slot, anchor_cols)
    ]
    return jnp.stack([routes.reshape(32, LANES), *ordered]).astype(jnp.int16)


def list_extents(lists):
    slot = lists[:, 1].astype(jnp.int32)
    late = jnp.arange(slot.shape[1], dtype=jnp.int32)[None, :, None] >= 16
    code = jnp.where(slot < 0, 0, (slot >> 10) + jnp.where(late, 8, 0))
    return jnp.max(code, axis=(1, 2))


def per_device(voltages, kernel, route_lists, row_members, row_counts, anchor_cols):
    chan_count = lax.axis_size("chan")
    row_count = lax.axis_size("row")
    group_size = voltages.shape[3]
    samples = voltages.shape[1]
    mine = lax.dynamic_index_in_dim(voltages, lax.axis_index("row"), 1, keepdims=False)
    mine = mine.reshape(chan_count, 2, group_size // LANES, LANES)
    volts = lax.all_to_all(mine, "chan", split_axis=0, concat_axis=0, tiled=True)
    lists = slab_lists(route_lists, row_members, row_counts, anchor_cols)
    lists = jnp.broadcast_to(lists[None], (row_count,) + lists.shape)
    volts, lists = lax.optimization_barrier((volts, lists))
    lists = lax.all_to_all(lists, "row", split_axis=0, concat_axis=0, tiled=True)
    wide, tall = stage_tables()
    power = sample_power(
        kernel[0],
        list_extents(lists),
        volts,
        lists,
        jnp.asarray(wide),
        jnp.asarray(tall),
    )
    power = power.reshape(row_count, NGRID // row_count, NGRID)
    power = lax.all_to_all(power, "row", split_axis=0, concat_axis=0, tiled=True)
    scale_factor = 1.0 / (group_size * chan_count * samples * KERNEL_SIDE * KERNEL_SIDE)
    sky_image = jnp.sum(power.astype(F32), axis=0) * scale_factor
    return sky_image.T[None]


def solution(mesh):
    in_specs = (
        P(None, None, None, "chan"),
        P("chan", None, None),
        P(None, "row", None),
        P("row", None),
        P("row"),
        P("row", None),
    )
    out_specs = P("chan", None, "row")
    return jax.shard_map(
        per_device, mesh=mesh, in_specs=in_specs, out_specs=out_specs, check_vma=False
    )
```

```python
import jax
import jax.numpy as jnp
import numpy as np
from jax import lax
from jax.experimental import pallas as pl
from jax.experimental.pallas import tpu as pltpu
from jax.sharding import PartitionSpec as P

NGRID = 1024
KERNEL_SIDE = 4
SLAB = 64
RADIX = 4
POINTS = NGRID // RADIX
LANES = 128
F32 = jnp.float32
BF16 = jnp.bfloat16


def stage_tables():
    n = np.arange(NGRID, dtype=np.int64)
    product = (n[:, None] * n[None, :POINTS]) % NGRID
    angles = product.astype(np.float32) * np.float32(-2.0 * np.pi / NGRID)
    cos = np.cos(angles).astype(np.float32)
    sin = np.sin(angles).astype(np.float32)
    parts = []
    for q in range(RADIX):
        c, s = cos[q::RADIX], sin[q::RADIX]
        parts.append(np.block([[c, s], [-s, c]]))
    table = np.stack(parts)
    return (
        np.ascontiguousarray(table.transpose(0, 2, 1)).astype(jnp.bfloat16),
        table.astype(jnp.bfloat16),
    )


def butterfly(re, im):
    ra, rb = re[0] + re[2], re[0] - re[2]
    rc, rd = re[1] + re[3], re[1] - re[3]
    ia, ib = im[0] + im[2], im[0] - im[2]
    ic, id_ = im[1] + im[3], im[1] - im[3]
    return (ra + rc, rb + id_, ra - rc, rb - id_), (ia + ic, ib - rd, ia - ic, ib + rd)


def pick(table_rows, index):
    return jnp.take_along_axis(table_rows, index, axis=1, mode="promise_in_bounds")


def sample_kernel(
    taps, extent, volts, lists, wide_from, tall_from, power_to, slots, bands, cells, aperture,
    spectrum, wide, tall, power, arrived, left_for,
):
    slabs = lists.shape[0]
    groups = volts.shape[0]
    slab_points = POINTS // slabs
    wide_copy = pltpu.make_async_copy(wide_from, wide, arrived.at[0])
    tall_copy = pltpu.make_async_copy(tall_from, tall, arrived.at[1])
    wide_copy.start()
    tall_copy.start()

    down = lax.broadcasted_iota(jnp.int32, (SLAB, 4 * SLAB), 0)
    across = lax.broadcasted_iota(jnp.int32, (SLAB, 4 * SLAB), 1)
    apart = RADIX * (down & 15) + (down >> 4)
    apart = apart - RADIX * (across & 15) - ((across >> 4) & 3)
    apart = apart + SLAB * ((across >> 6) & 1)
    for kx in range(KERNEL_SIDE):
        tap = jnp.zeros((SLAB, 4 * SLAB), F32)
        for ky in range(KERNEL_SIDE):
            tap = jnp.where(apart == ky, taps[ky, kx], tap)
        high = tap.astype(BF16).astype(F32)
        bands[kx * SLAB : (kx + 1) * SLAB, :] = jnp.where(
            across < 2 * SLAB, high, tap - high
        ).astype(BF16)
    cells[2] = jnp.zeros(cells.shape[1:], BF16)

    sub = lax.broadcasted_iota(jnp.int32, (8, LANES), 0)
    lane = lax.broadcasted_iota(jnp.int32, (8, LANES), 1)
    own_row = sub == lane >> 4
    first_lane = lax.broadcasted_iota(jnp.int32, (SLAB, POINTS), 1) == 0

    row_of = lax.broadcasted_iota(jnp.int32, (32, 2 * LANES), 0)
    lane_of = lax.broadcasted_iota(jnp.int32, (LANES, 2 * LANES), 0).astype(BF16)

    def gather_pair(pair, carry):
        first, second = 2 * pair, 2 * pair + 1
        routes = [lists[r, 0].astype(jnp.int32) for r in (first, second)]
        last = jnp.maximum(extent[first] & 3, extent[second] & 3)
        for s in (0, 2):

            @pl.when(last >= s)
            def _():
                for g in range(2 * groups):
                    k = 8 * s + g
                    route = jnp.concatenate([a[k : k + 1, :] for a in routes], axis=1)
                    lane_spot = (route & (LANES - 1)).astype(F32).astype(BF16)
                    onehot = jnp.where(lane_of == lane_spot, BF16(1), BF16(0))
                    rows = jnp.dot(
                        volts[g % groups].reshape(64, LANES),
                        onehot,
                        preferred_element_type=F32,
                    )
                    hit = row_of == (route >> 7)
                    for i in range(2):
                        entry = jnp.sum(
                            jnp.where(hit, rows[32 * i : 32 * i + 32], 0.0),
                            axis=0,
                            keepdims=True,
                        )
                        slots[i, first, k : k + 1, :] = entry[:, :LANES]
                        slots[i, second, k : k + 1, :] = entry[:, LANES:]

        return carry

    lax.fori_loop(0, slabs // 2, gather_pair, 0)

    def convolve(r):
        here = lax.rem(r + 3, 3)
        before = lax.rem(r + 2, 3)
        for i in range(2):
            sums = []
            for q in range(RADIX):
                rows = [cells[here, 2 * q + i], cells[before, 2 * q + i]]
                sums.append(
                    jnp.dot(
                        bands[...],
                        jnp.concatenate(rows + rows, axis=0),
                        preferred_element_type=F32,
                    )
                )
            for qx in range(RADIX):
                terms = [
                    sums[(qx - kx) % RADIX][kx * SLAB : (kx + 1) * SLAB]
                    for kx in range(KERNEL_SIDE)
                ]
                total = sum(terms[1 : qx + 1], terms[0])
                if qx < KERNEL_SIDE - 1:
                    spill = sum(terms[qx + 2 :], terms[qx + 1])
                    spill = pltpu.roll(spill, 1, 1)
                    total = total + jnp.where(first_lane, 0.0, spill)
                total = total.astype(BF16)
                at = (2 * qx + i) * POINTS
                for qy in range(RADIX):
                    row = pl.multiple_of(qy * POINTS + slab_points * jnp.maximum(r, 0), 16)
                    aperture[pl.ds(row, 16), at : at + POINTS] = total[
                        16 * qy : 16 * qy + 16
                    ]

    def grid_chunks(r, chunks, list_rows):
        convolve(r - 1)
        place = lax.rem(r, 3)
        size = 8 * chunks
        members = lists[r, 1].astype(jnp.int32)[:size]
        columns = lists[r, 2].astype(jnp.int32)[:size]
        member_lane = members & (LANES - 1)
        member_row = members >> 7
        values = [jnp.zeros((size, LANES), F32)] * 2
        for k in range(list_rows):
            hit = member_row == k
            for i in range(2):
                row = jnp.broadcast_to(slots[i, r, k : k + 1, :], (size, LANES))
                values[i] = jnp.where(hit, pick(row, member_lane), values[i])
        kind = (columns & (RADIX - 1)) + RADIX * (columns >> 9)
        point = ((columns >> 2) & (LANES - 1)).astype(F32)
        cell = lax.broadcasted_iota(jnp.int32, (LANES, chunks * LANES), 0).astype(BF16)
        for qy in range(RADIX):
            placed = []
            for h in range(2):
                at = [8 * c + 2 * qy + h for c in range(chunks)]
                kinds = [
                    jnp.where(
                        own_row, jnp.broadcast_to(kind[a : a + 1, :], (8, LANES)), -1
                    )
                    for a in at
                ]
                spread = [
                    [jnp.broadcast_to(v[a : a + 1, :], (8, LANES)) for a in at]
                    for v in values
                ]
                left = jnp.concatenate(
                    [
                        jnp.concatenate(
                            [
                                jnp.where(kinds[c] == plane, spread[i][c], 0.0)
                                for c in range(chunks)
                            ],
                            axis=1,
                        )
                        for plane in range(2 * RADIX)
                        for i in range(2)
                    ],
                    axis=0,
                ).astype(BF16)
                spot = jnp.concatenate([point[a : a + 1, :] for a in at], axis=1)
                onehot = jnp.where(cell == spot.astype(BF16), BF16(1), BF16(0))
                placed.append(
                    lax.dot_general(
                        left,
                        onehot,
                        (((1,), (1,)), ((), ())),
                        preferred_element_type=F32,
                    )
                )
            for half in range(2):
                for plane in range(2 * RADIX):
                    a = (half * 2 * RADIX + plane) * 8
                    cells[
                        place,
                        plane,
                        16 * qy : 16 * qy + 16,
                        half * LANES : (half + 1) * LANES,
                    ] = jnp.concatenate([p[a : a + 8, :] for p in placed], axis=0).astype(
                        BF16
                    )

    def grid_slab(r, carry):
        @pl.when(extent[r] < 4)
        def _():
            grid_chunks(r, 2, 16)

        @pl.when(extent[r] >= 4)
        def _():
            grid_chunks(r, 4, 32)

        return carry

    lax.fori_loop(0, slabs, grid_slab, 0)
    convolve(slabs - 1)

    def row_transform(qy, carry):
        rows = pl.ds(pl.multiple_of(qy * POINTS, POINTS), POINTS)
        parts = [
            lax.dot_general(
                wide[q],
                aperture[rows, 2 * q * POINTS : 2 * (q + 1) * POINTS],
                (((1,), (1,)), ((), ())),
                preferred_element_type=F32,
            )
            for q in range(RADIX)
        ]
        re, im = butterfly(
            [part[:POINTS] for part in parts], [part[POINTS:] for part in parts]
        )
        at = pl.multiple_of(qy * 2 * POINTS, 2 * POINTS)
        for m in range(RADIX):
            spectrum[m * POINTS : (m + 1) * POINTS, pl.ds(at, POINTS)] = re[m].astype(
                BF16
            )
            spectrum[
                m * POINTS : (m + 1) * POINTS, pl.ds(at + POINTS, POINTS)
            ] = im[m].astype(BF16)
        return carry

    wide_copy.wait()
    lax.fori_loop(0, RADIX, row_transform, 0, unroll=True)

    def hand_over(n):
        rows = pl.ds(n * POINTS, POINTS)
        return pltpu.make_async_copy(power.at[rows], power_to.at[rows], left_for.at[n])

    def column_transform(n, carry):
        rows = pl.ds(n * POINTS, POINTS)
        parts = [
            jnp.dot(
                spectrum[rows, 2 * q * POINTS : 2 * (q + 1) * POINTS],
                tall[q],
                preferred_element_type=F32,
            )
            for q in range(RADIX)
        ]
        re, im = butterfly(
            [part[:, :POINTS] for part in parts], [part[:, POINTS:] for part in parts]
        )
        for m in range(RADIX):
            power[rows, m * POINTS : (m + 1) * POINTS] = (
                re[m] * re[m] + im[m] * im[m]
            ).astype(BF16)
        return carry

    tall_copy.wait()
    for n in range(RADIX):
        column_transform(n, 0)
        hand_over(n).start()
    for n in range(RADIX):
        hand_over(n).wait()


def sample_power(taps, extent, volts, lists, wide, tall):
    return pl.pallas_call(
        sample_kernel,
        out_shape=jax.ShapeDtypeStruct((NGRID, NGRID), BF16),
        in_specs=[pl.BlockSpec(memory_space=pltpu.SMEM)] * 2
        + [pl.BlockSpec(memory_space=pltpu.VMEM)] * 2
        + [pl.BlockSpec(memory_space=pl.ANY)] * 2,
        out_specs=pl.BlockSpec(memory_space=pl.ANY),
        scratch_shapes=[
            pltpu.VMEM((2, lists.shape[0], 32, LANES), F32),
            pltpu.VMEM((4 * SLAB, 4 * SLAB), BF16),
            pltpu.VMEM((3, 2 * RADIX, SLAB, POINTS), BF16),
            pltpu.VMEM((NGRID, 2 * NGRID), BF16),
            pltpu.VMEM((NGRID, 2 * NGRID), BF16),
            pltpu.VMEM(wide.shape, BF16),
            pltpu.VMEM(tall.shape, BF16),
            pltpu.VMEM((NGRID, NGRID), BF16),
            pltpu.SemaphoreType.DMA((2,)),
            pltpu.SemaphoreType.DMA((RADIX,)),
        ],
        compiler_params=pltpu.CompilerParams(vmem_limit_bytes=56 * 2**20),
    )(taps, extent, volts, lists, wide, tall)


def slab_lists(route_lists, row_members, row_counts, anchor_cols):
    routes = route_lists[:, 0, :].reshape(8, 4, LANES).transpose(1, 0, 2)
    slot = ((row_members >> 7) & 3) * 1024 + (row_members >> 9) * LANES
    slot = slot + (row_members & (LANES - 1))
    live = jnp.arange(row_members.shape[1], dtype=jnp.int32)[None, :] < row_counts[:, None]
    slot = jnp.where(live, slot, -1)
    ordered = [
        a.reshape(2, 8, RADIX, 4, 16).transpose(3, 2, 0, 1, 4).reshape(32, LANES)
        for a in (slot, anchor_cols)
    ]
    return jnp.stack([routes.reshape(32, LANES), *ordered]).astype(jnp.int16)


def list_extents(lists):
    slot = lists[:, 1].astype(jnp.int32)
    top = jnp.max(slot, axis=(1, 2))
    late = jnp.max(slot[:, 16:], axis=(1, 2))
    wide = (top >= 2048) | (late >= 0)
    return (jnp.maximum(top, 0) >> 10) + jnp.where(wide, 4, 0)


def per_device(voltages, kernel, route_lists, row_members, row_counts, anchor_cols):
    chan_count = lax.axis_size("chan")
    row_count = lax.axis_size("row")
    group_size = voltages.shape[3]
    samples = voltages.shape[1]
    mine = lax.dynamic_index_in_dim(voltages, lax.axis_index("row"), 1, keepdims=False)
    mine = mine.reshape(chan_count, 2, group_size // LANES, LANES)
    volts = lax.all_to_all(mine, "chan", split_axis=0, concat_axis=0, tiled=True)
    lists = slab_lists(route_lists, row_members, row_counts, anchor_cols)
    lists = jnp.broadcast_to(lists[None], (row_count,) + lists.shape)
    volts, lists = lax.optimization_barrier((volts, lists))
    lists = lax.all_to_all(lists, "row", split_axis=0, concat_axis=0, tiled=True)
    wide, tall = stage_tables()
    power = sample_power(
        kernel[0],
        list_extents(lists),
        volts,
        lists,
        jnp.asarray(wide),
        jnp.asarray(tall),
    )
    power = power.reshape(row_count, NGRID // row_count, NGRID)
    power = lax.all_to_all(power, "row", split_axis=0, concat_axis=0, tiled=True)
    scale_factor = 1.0 / (group_size * chan_count * samples * KERNEL_SIDE * KERNEL_SIDE)
    sky_image = jnp.sum(power.astype(F32), axis=0) * scale_factor
    return sky_image.T[None]


def solution(mesh):
    in_specs = (
        P(None, None, None, "chan"),
        P("chan", None, None),
        P(None, "row", None),
        P("row", None),
        P("row"),
        P("row", None),
    )
    out_specs = P("chan", None, "row")
    return jax.shard_map(
        per_device, mesh=mesh, in_specs=in_specs, out_specs=out_specs, check_vma=False
    )
```

```python
import jax
import jax.numpy as jnp
import numpy as np
from jax import lax
from jax.experimental import pallas as pl
from jax.experimental.pallas import tpu as pltpu
from jax.sharding import PartitionSpec as P

NGRID = 1024
KERNEL_SIDE = 4
SLAB = 64
RADIX = 4
POINTS = NGRID // RADIX
LANES = 128
F32 = jnp.float32
BF16 = jnp.bfloat16


def stage_tables():
    n = np.arange(NGRID, dtype=np.int64)
    product = (n[:, None] * n[None, :POINTS]) % NGRID
    angles = product.astype(np.float32) * np.float32(-2.0 * np.pi / NGRID)
    cos = np.cos(angles).astype(np.float32)
    sin = np.sin(angles).astype(np.float32)
    parts = []
    for q in range(RADIX):
        c, s = cos[q::RADIX], sin[q::RADIX]
        parts.append(np.block([[c, s], [-s, c]]))
    table = np.stack(parts)
    return (
        np.ascontiguousarray(table.transpose(0, 2, 1)).astype(jnp.bfloat16),
        table.astype(jnp.bfloat16),
    )


def butterfly(re, im):
    ra, rb = re[0] + re[2], re[0] - re[2]
    rc, rd = re[1] + re[3], re[1] - re[3]
    ia, ib = im[0] + im[2], im[0] - im[2]
    ic, id_ = im[1] + im[3], im[1] - im[3]
    return (ra + rc, rb + id_, ra - rc, rb - id_), (ia + ic, ib - rd, ia - ic, ib + rd)


def pick(table_rows, index):
    return jnp.take_along_axis(table_rows, index, axis=1, mode="promise_in_bounds")


def sample_kernel(
    taps, extent, volts, lists, wide_from, tall_from, power_to, slots, bands, cells, aperture,
    spectrum, wide, tall, power, arrived, left_for,
):
    slabs = lists.shape[0]
    groups = volts.shape[0]
    slab_points = POINTS // slabs
    wide_copy = pltpu.make_async_copy(wide_from, wide, arrived.at[0])
    tall_copy = pltpu.make_async_copy(tall_from, tall, arrived.at[1])
    wide_copy.start()
    tall_copy.start()

    down = lax.broadcasted_iota(jnp.int32, (SLAB, 4 * SLAB), 0)
    across = lax.broadcasted_iota(jnp.int32, (SLAB, 4 * SLAB), 1)
    apart = RADIX * (down & 15) + (down >> 4)
    apart = apart - RADIX * (across & 15) - ((across >> 4) & 3)
    apart = apart + SLAB * ((across >> 6) & 1)
    for kx in range(KERNEL_SIDE):
        tap = jnp.zeros((SLAB, 4 * SLAB), F32)
        for ky in range(KERNEL_SIDE):
            tap = jnp.where(apart == ky, taps[ky, kx], tap)
        high = tap.astype(BF16).astype(F32)
        bands[kx * SLAB : (kx + 1) * SLAB, :] = jnp.where(
            across < 2 * SLAB, high, tap - high
        ).astype(BF16)
    cells[2] = jnp.zeros(cells.shape[1:], BF16)

    sub = lax.broadcasted_iota(jnp.int32, (8, LANES), 0)
    lane = lax.broadcasted_iota(jnp.int32, (8, LANES), 1)
    own_row = sub == lane >> 4
    first_lane = lax.broadcasted_iota(jnp.int32, (SLAB, POINTS), 1) == 0

    row_of = lax.broadcasted_iota(jnp.int32, (32, 2 * LANES), 0)
    lane_of = lax.broadcasted_iota(jnp.int32, (LANES, 2 * LANES), 0).astype(BF16)

    def gather_pair(pair, carry, s):
        first, second = 2 * pair, 2 * pair + 1
        routes = [lists[r, 0].astype(jnp.int32) for r in (first, second)]
        last = jnp.maximum(extent[first] & 3, extent[second] & 3)
        if True:

            def look_up():
                for g in range(2 * groups):
                    k = 8 * s + g
                    route = jnp.concatenate([a[k : k + 1, :] for a in routes], axis=1)
                    lane_spot = (route & (LANES - 1)).astype(F32).astype(BF16)
                    onehot = jnp.where(lane_of == lane_spot, BF16(1), BF16(0))
                    rows = jnp.dot(
                        volts[g % groups].reshape(64, LANES),
                        onehot,
                        preferred_element_type=F32,
                    )
                    hit = row_of == (route >> 7)
                    for i in range(2):
                        entry = jnp.sum(
                            jnp.where(hit, rows[32 * i : 32 * i + 32], 0.0),
                            axis=0,
                            keepdims=True,
                        )
                        slots[i, first, k : k + 1, :] = entry[:, :LANES]
                        slots[i, second, k : k + 1, :] = entry[:, LANES:]

        if s == 0:
            look_up()
        else:
            pl.when(last >= s)(look_up)
        return carry

    lax.fori_loop(0, slabs // 2, lambda n, c: gather_pair(n, c, 0), 0, unroll=2)
    lax.fori_loop(0, slabs // 2, lambda n, c: gather_pair(n, c, 2), 0)

    def convolve(r):
        here = lax.rem(r + 3, 3)
        before = lax.rem(r + 2, 3)
        for i in range(2):
            sums = []
            for q in range(RADIX):
                rows = [cells[here, 2 * q + i], cells[before, 2 * q + i]]
                sums.append(
                    jnp.dot(
                        bands[...],
                        jnp.concatenate(rows + rows, axis=0),
                        preferred_element_type=F32,
                    )
                )
            for qx in range(RADIX):
                terms = [
                    sums[(qx - kx) % RADIX][kx * SLAB : (kx + 1) * SLAB]
                    for kx in range(KERNEL_SIDE)
                ]
                total = sum(terms[1 : qx + 1], terms[0])
                if qx < KERNEL_SIDE - 1:
                    spill = sum(terms[qx + 2 :], terms[qx + 1])
                    spill = pltpu.roll(spill, 1, 1)
                    total = total + jnp.where(first_lane, 0.0, spill)
                total = total.astype(BF16)
                at = (2 * qx + i) * POINTS
                for qy in range(RADIX):
                    row = pl.multiple_of(qy * POINTS + slab_points * jnp.maximum(r, 0), 16)
                    aperture[pl.ds(row, 16), at : at + POINTS] = total[
                        16 * qy : 16 * qy + 16
                    ]

    def grid_chunks(r, chunks, list_rows):
        convolve(r - 1)
        place = lax.rem(r, 3)
        size = 8 * chunks
        members = lists[r, 1].astype(jnp.int32)[:size]
        columns = lists[r, 2].astype(jnp.int32)[:size]
        member_lane = members & (LANES - 1)
        member_row = members >> 7
        values = [jnp.zeros((size, LANES), F32)] * 2
        for k in range(list_rows):
            hit = member_row == k
            for i in range(2):
                row = jnp.broadcast_to(slots[i, r, k : k + 1, :], (size, LANES))
                values[i] = jnp.where(hit, pick(row, member_lane), values[i])
        kind = (columns & (RADIX - 1)) + RADIX * (columns >> 9)
        point = ((columns >> 2) & (LANES - 1)).astype(F32)
        cell = lax.broadcasted_iota(jnp.int32, (LANES, chunks * LANES), 0).astype(BF16)
        for qy in range(RADIX):
            placed = []
            for h in range(2):
                at = [8 * c + 2 * qy + h for c in range(chunks)]
                kinds = [
                    jnp.where(
                        own_row, jnp.broadcast_to(kind[a : a + 1, :], (8, LANES)), -1
                    )
                    for a in at
                ]
                spread = [
                    [jnp.broadcast_to(v[a : a + 1, :], (8, LANES)) for a in at]
                    for v in values
                ]
                left = jnp.concatenate(
                    [
                        jnp.concatenate(
                            [
                                jnp.where(kinds[c] == plane, spread[i][c], 0.0)
                                for c in range(chunks)
                            ],
                            axis=1,
                        )
                        for plane in range(2 * RADIX)
                        for i in range(2)
                    ],
                    axis=0,
                ).astype(BF16)
                spot = jnp.concatenate([point[a : a + 1, :] for a in at], axis=1)
                onehot = jnp.where(cell == spot.astype(BF16), BF16(1), BF16(0))
                placed.append(
                    lax.dot_general(
                        left,
                        onehot,
                        (((1,), (1,)), ((), ())),
                        preferred_element_type=F32,
                    )
                )
            for half in range(2):
                for plane in range(2 * RADIX):
                    a = (half * 2 * RADIX + plane) * 8
                    cells[
                        place,
                        plane,
                        16 * qy : 16 * qy + 16,
                        half * LANES : (half + 1) * LANES,
                    ] = jnp.concatenate([p[a : a + 8, :] for p in placed], axis=0).astype(
                        BF16
                    )

    def grid_slab(r, carry):
        @pl.when(extent[r] < 4)
        def _():
            grid_chunks(r, 2, 16)

        @pl.when(extent[r] >= 4)
        def _():
            grid_chunks(r, 4, 32)

        return carry

    lax.fori_loop(0, slabs, grid_slab, 0)
    convolve(slabs - 1)

    def row_transform(qy, carry):
        rows = pl.ds(pl.multiple_of(qy * POINTS, POINTS), POINTS)
        parts = [
            lax.dot_general(
                wide[q],
                aperture[rows, 2 * q * POINTS : 2 * (q + 1) * POINTS],
                (((1,), (1,)), ((), ())),
                preferred_element_type=F32,
            )
            for q in range(RADIX)
        ]
        re, im = butterfly(
            [part[:POINTS] for part in parts], [part[POINTS:] for part in parts]
        )
        at = pl.multiple_of(qy * 2 * POINTS, 2 * POINTS)
        for m in range(RADIX):
            spectrum[m * POINTS : (m + 1) * POINTS, pl.ds(at, POINTS)] = re[m].astype(
                BF16
            )
            spectrum[
                m * POINTS : (m + 1) * POINTS, pl.ds(at + POINTS, POINTS)
            ] = im[m].astype(BF16)
        return carry

    wide_copy.wait()
    lax.fori_loop(0, RADIX, row_transform, 0, unroll=True)

    def hand_over(n):
        rows = pl.ds(n * POINTS, POINTS)
        return pltpu.make_async_copy(power.at[rows], power_to.at[rows], left_for.at[n])

    def column_transform(n, carry):
        rows = pl.ds(n * POINTS, POINTS)
        parts = [
            jnp.dot(
                spectrum[rows, 2 * q * POINTS : 2 * (q + 1) * POINTS],
                tall[q],
                preferred_element_type=F32,
            )
            for q in range(RADIX)
        ]
        re, im = butterfly(
            [part[:, :POINTS] for part in parts], [part[:, POINTS:] for part in parts]
        )
        for m in range(RADIX):
            power[rows, m * POINTS : (m + 1) * POINTS] = (
                re[m] * re[m] + im[m] * im[m]
            ).astype(BF16)
        return carry

    tall_copy.wait()
    for n in range(RADIX):
        column_transform(n, 0)
        hand_over(n).start()
    for n in range(RADIX):
        hand_over(n).wait()


def sample_power(taps, extent, volts, lists, wide, tall):
    return pl.pallas_call(
        sample_kernel,
        out_shape=jax.ShapeDtypeStruct((NGRID, NGRID), BF16),
        in_specs=[pl.BlockSpec(memory_space=pltpu.SMEM)] * 2
        + [pl.BlockSpec(memory_space=pltpu.VMEM)] * 2
        + [pl.BlockSpec(memory_space=pl.ANY)] * 2,
        out_specs=pl.BlockSpec(memory_space=pl.ANY),
        scratch_shapes=[
            pltpu.VMEM((2, lists.shape[0], 32, LANES), F32),
            pltpu.VMEM((4 * SLAB, 4 * SLAB), BF16),
            pltpu.VMEM((3, 2 * RADIX, SLAB, POINTS), BF16),
            pltpu.VMEM((NGRID, 2 * NGRID), BF16),
            pltpu.VMEM((NGRID, 2 * NGRID), BF16),
            pltpu.VMEM(wide.shape, BF16),
            pltpu.VMEM(tall.shape, BF16),
            pltpu.VMEM((NGRID, NGRID), BF16),
            pltpu.SemaphoreType.DMA((2,)),
            pltpu.SemaphoreType.DMA((RADIX,)),
        ],
        compiler_params=pltpu.CompilerParams(vmem_limit_bytes=56 * 2**20),
    )(taps, extent, volts, lists, wide, tall)


def slab_lists(route_lists, row_members, row_counts, anchor_cols):
    routes = route_lists[:, 0, :].reshape(8, 4, LANES).transpose(1, 0, 2)
    slot = ((row_members >> 7) & 3) * 1024 + (row_members >> 9) * LANES
    slot = slot + (row_members & (LANES - 1))
    live = jnp.arange(row_members.shape[1], dtype=jnp.int32)[None, :] < row_counts[:, None]
    slot = jnp.where(live, slot, -1)
    ordered = [
        a.reshape(2, 8, RADIX, 4, 16).transpose(3, 2, 0, 1, 4).reshape(32, LANES)
        for a in (slot, anchor_cols)
    ]
    return jnp.stack([routes.reshape(32, LANES), *ordered]).astype(jnp.int16)


def list_extents(lists):
    slot = lists[:, 1].astype(jnp.int32)
    top = jnp.max(slot, axis=(1, 2))
    late = jnp.max(slot[:, 16:], axis=(1, 2))
    wide = (top >= 2048) | (late >= 0)
    return (jnp.maximum(top, 0) >> 10) + jnp.where(wide, 4, 0)


def per_device(voltages, kernel, route_lists, row_members, row_counts, anchor_cols):
    chan_count = lax.axis_size("chan")
    row_count = lax.axis_size("row")
    group_size = voltages.shape[3]
    samples = voltages.shape[1]
    mine = lax.dynamic_index_in_dim(voltages, lax.axis_index("row"), 1, keepdims=False)
    mine = mine.reshape(chan_count, 2, group_size // LANES, LANES)
    volts = lax.all_to_all(mine, "chan", split_axis=0, concat_axis=0, tiled=True)
    lists = slab_lists(route_lists, row_members, row_counts, anchor_cols)
    lists = jnp.broadcast_to(lists[None], (row_count,) + lists.shape)
    volts, lists = lax.optimization_barrier((volts, lists))
    lists = lax.all_to_all(lists, "row", split_axis=0, concat_axis=0, tiled=True)
    wide, tall = stage_tables()
    power = sample_power(
        kernel[0],
        list_extents(lists),
        volts,
        lists,
        jnp.asarray(wide),
        jnp.asarray(tall),
    )
    power = power.reshape(row_count, NGRID // row_count, NGRID)
    power = lax.all_to_all(power, "row", split_axis=0, concat_axis=0, tiled=True)
    scale_factor = 1.0 / (group_size * chan_count * samples * KERNEL_SIDE * KERNEL_SIDE)
    sky_image = jnp.sum(power.astype(F32), axis=0) * scale_factor
    return sky_image.T[None]


def solution(mesh):
    in_specs = (
        P(None, None, None, "chan"),
        P("chan", None, None),
        P(None, "row", None),
        P("row", None),
        P("row"),
        P("row", None),
    )
    out_specs = P("chan", None, "row")
    return jax.shard_map(
        per_device, mesh=mesh, in_specs=in_specs, out_specs=out_specs, check_vma=False
    )
```
